1024 devices in a mesh: replica: 16 (over z_lo, core), shard: 64 (over x, z_hi, y).
Axes of the slice: x: 4, y: 4, z: 32 (z_hi: 4, z_lo: 8; z = z_hi * 8 + z_lo), core: 2. Of those that a mesh axis runs over, the one named last changes fastest.
Arguments:
- emb_table: float32 [262144, 128], P('shard'), may hold values from -2 to 2
- active_blocks: int32 [16, 64, 16], P(None, 'shard'), may hold values from 0 to 255, as said below
- hit_shards: int32 [16, 4, 16384, 2], P('replica', None, 'shard'), may hold values from 0 to 63, all different within a row; in each aligned block of 256 rows (0 to 255, 256 to 511, ..., all dimensions but the last counted through in order) at most 12 rows name the same one
- lookup_slot: int32 [16, 4, 16384, 2, 4], P('replica', None, 'shard'), may hold values from 0 to 15
- lookup_offset: int32 [16, 4, 16384, 2, 4], P('replica', None, 'shard'), may hold values from 0 to 15
- block_weight: float32 [16, 4, 64, 16], P('replica', None, 'shard'), may hold values from 0.25 to 2
- dense_feat: bfloat16 [16, 4, 16384, 128], P('replica', None, 'shard'), may hold values from -6 to 6
- labels: int32 [16, 4, 16384], P('replica', None, 'shard'), may hold values from 0 to 1
Outputs:
- new_table: float32 [262144, 128], P('shard')
- step_logits: float32 [16, 4, 16384], P('replica', None, 'shard')
The draws below stay inside these ranges and needn't reach their ends.
Inputs may be any that keep to these rules, and one draw needn't show every extreme that they name: `hit_shards`: in each aligned block of 256 rows (the samples of one device in one step) no shard is named by more than 12 hits, and a sample's 2 shards differ. `active_blocks`: the 16 blocks of one group and shard differ and stand in ascending order.
All inputs are finite; a program needn't handle non-finite values.
Results may differ from the reference program's by a relative error of at most 0.0016.
Values may be sent and summed in bfloat16 or wider, within the bound.
No kernel may reach another device: no remote copies, remote signals or barrier semaphores. Data moves between devices by JAX's collectives and lax.ppermute only.
A program may use at most 32 MiB of HBM per device.

```python
import math
import jax
import jax.numpy as jnp
import numpy as np
from jax import lax

E = 128
BLK = 16
ACT = 16
LOOK = 4
HITS = 2
STEPS = 4
ROWS_DEV = 4096
SAMP_DEV = 256
BLOCKS_DEV = 256
ROWS = 262144
SAMP = 16384
CAP = 12
GROUPS = 16
N_REPLICA = 16
N_SHARD = 64


def draw_active_blocks(key, part):
    key = jax.random.fold_in(key, 5)
    scores = jax.random.randint(key, (N_REPLICA, N_SHARD, BLOCKS_DEV), 0, 1 << 20) * BLOCKS_DEV + jnp.arange(BLOCKS_DEV, dtype=jnp.int32)
    scores = scores.at[0, 0, 0].set(-2).at[0, 0, BLOCKS_DEV - 1].set(-1)
    chosen = jnp.argsort(scores, axis=-1)[:, :, :ACT]
    return jnp.sort(chosen, axis=-1).astype(jnp.int32)


def touch_ends(result, own_key, low, largest):
    dims = result.shape
    spot = [jax.random.randint(jax.random.fold_in(own_key, axis), (), 0, dims[axis]) for axis in range(len(dims))]
    result = result.at[tuple(spot)].set(low)
    longest = dims.index(max(dims))
    spot[longest] = (spot[longest] + 1) % dims[longest]
    return result.at[tuple(spot)].set(largest)


def shard_levels(rng, dims, split, least, largest):
    gain, own = 1.0, jax.random.fold_in(rng, 6)
    for axis_at, blocks in split:
        heights = jnp.exp(jax.random.uniform(jax.random.fold_in(own, axis_at), (blocks,), jnp.float32, least / len(split), largest / len(split)))
        gain = gain * jnp.repeat(heights, dims[axis_at] // blocks).reshape([-1 if axis == axis_at else 1 for axis in range(len(dims))])
    return gain


def shared_out(own_key, own, number, rows, count, top, bound, lean):
    ranking = jax.random.permutation(own_key, count)
    heavy_load, usual = portions_of(count, rows * top, bound, lean, True), portions_of(count, rows * top, bound, lean, False)
    places = jnp.arange(count)

    def named(lengths, offset_by):
        used = int((lengths > 0).sum())
        fixed = max(1, used // 4)
        passed = fixed + (places - fixed + offset_by * (used - fixed)) % max(1, count - fixed)
        return jnp.zeros((count,), jnp.int32).at[ranking[jnp.where(places < fixed, places, passed)]].set(jnp.asarray(lengths, jnp.int32))

    lengths = jnp.where(number % 4 == 0, named(heavy_load, number // 4), named(usual, number - number // 4 - 1))
    mixed = jax.random.permutation(jax.random.fold_in(own, 3), count)
    source_of, receiver = mixed[0:count // 2 * 2:2], mixed[1:count // 2 * 2:2]
    margin = jnp.minimum(lengths[source_of] - 1, bound - lengths[receiver]) // 2
    margin = jnp.where((source_of == ranking[0]) | (receiver == ranking[0]) | (lengths[receiver] == 0), 0, jnp.maximum(margin, 0))
    passed = jax.random.randint(jax.random.fold_in(own, 4), (count // 2,), 0, 1 << 20) % (margin + 1)
    lengths = lengths.at[source_of].add(-passed).at[receiver].add(passed)
    items = jnp.searchsorted(jnp.cumsum(lengths), jnp.arange(rows * top), side="right").astype(jnp.int32)
    listing = items.reshape(top, rows).T
    listing = listing[jax.random.permutation(jax.random.fold_in(own, 1), rows)]
    offset_by = jax.random.randint(jax.random.fold_in(own, 2), (rows, 1), 0, top)
    return jnp.take_along_axis(listing, (jnp.arange(top)[None, :] + offset_by) % top, axis=1)


def portions_of(number_of, total, most, slope, full):
    weights = [(1 << 20) // math.isqrt(grade ** slope) + 1 for grade in range(1, number_of + 1)]
    largest = most if full else min(most, max(-(-total // number_of), total * weights[0] // sum(weights)))
    least = 1 if total - largest >= number_of - 1 else 0
    counts, surplus = [largest] + [least] * (number_of - 1), total - largest - least * (number_of - 1)
    while surplus > 0:
        free = [i for i in range(1, number_of) if counts[i] < largest] or [i for i in range(1, number_of) if counts[i] < most]
        pool, remaining = sum([weights[i] for i in free]), surplus
        for i in free:
            addition = min(most - counts[i], max(1, remaining * weights[i] // pool), surplus)
            counts[i] = counts[i] + addition
            surplus = surplus - addition
    return np.array(counts)


def scatter_about(stream_key, extent, spread, reach, cuts=(), kind=jnp.bfloat16):
    factor_of = shard_levels(stream_key, extent, cuts, -0.22, 0.18) if cuts else 1.0
    values = jax.random.normal(stream_key, extent, jnp.float32) * spread * factor_of
    return jnp.minimum(jnp.maximum(values, -reach), reach).astype(kind)


def setup_inputs(seed: int = 0) -> dict:
    key_list = jax.random.split(jax.random.key(seed), 9)
    emb_table = scatter_about(key_list[0], (ROWS, E), 0.35, 2.0, ((0, 64),), jnp.float32)
    active_blocks = draw_active_blocks(jax.random.fold_in(key_list[8], 71), 0)
    hit_shards_keys = jax.random.split(jax.random.fold_in(key_list[2], 1), GROUPS * STEPS * SAMP // SAMP_DEV)
    hit_shards_turns = jax.random.permutation(jax.random.fold_in(key_list[2], 3), GROUPS * STEPS * SAMP // SAMP_DEV)
    hit_shards = jax.vmap(lambda own, number: shared_out(jax.random.fold_in(key_list[2], 2), own, number, SAMP_DEV, N_SHARD, HITS, CAP, 2))(hit_shards_keys, hit_shards_turns).reshape((GROUPS, STEPS, SAMP, HITS))
    lookup_slot = touch_ends(jax.random.randint(key_list[3], (GROUPS, STEPS, SAMP, HITS, LOOK), 0, ACT), jax.random.fold_in(key_list[3], 1), 0, ACT - 1).astype(jnp.int32)
    lookup_offset = touch_ends(jax.random.randint(key_list[4], (GROUPS, STEPS, SAMP, HITS, LOOK), 0, BLK), jax.random.fold_in(key_list[4], 1), 0, BLK - 1).astype(jnp.int32)
    block_weight = jnp.clip(jnp.exp(math.log(2.0) - 2.0794415 * jax.random.uniform(key_list[5], (GROUPS, STEPS, N_SHARD, ACT), jnp.float32) ** shard_levels(key_list[5], (GROUPS, STEPS, N_SHARD, ACT), ((0, 16), (2, 64)), -0.2, 0.2)), 0.25, 2.0)
    dense_feat = scatter_about(key_list[6], (GROUPS, STEPS, SAMP, E), 1.0, 6.0, ((0, 16), (2, 64)))
    labels = touch_ends(jax.random.randint(key_list[7], (GROUPS, STEPS, SAMP), 0, 2), jax.random.fold_in(key_list[7], 1), 0, 1).astype(jnp.int32)
    return {"emb_table": emb_table, "active_blocks": active_blocks, "hit_shards": hit_shards, "lookup_slot": lookup_slot, "lookup_offset": lookup_offset, "block_weight": block_weight, "dense_feat": dense_feat, "labels": labels}


step_rate = 1.0


def group_round(emb_table, blocks, hit_shards, lookup_slot, lookup_offset, block_weight, dense_feat, labels):
    act_rows = ACT * BLK
    within = jnp.arange(BLK, dtype=jnp.int32)
    local_rows = (blocks[:, :, None] * BLK + within[None, None, :]).reshape(N_SHARD, act_rows)
    row_index = (jnp.arange(N_SHARD, dtype=jnp.int32)[:, None] * ROWS_DEV + local_rows).reshape(-1).astype(jnp.int32)
    initial = emb_table[row_index]
    current = initial
    inv_root = E ** -0.5
    logit_list = []
    for step_no in range(STEPS):
        shard_ids = hit_shards[step_no]
        slot_ids = lookup_slot[step_no]
        flat_ids = (shard_ids[:, :, None] * act_rows + slot_ids * BLK + lookup_offset[step_no]).astype(jnp.int32)
        weights = block_weight[step_no][shard_ids[:, :, None], slot_ids]
        gathered = current[flat_ids]
        pooled = jnp.sum(weights[..., None] * gathered, axis=(1, 2))
        features = dense_feat[step_no].astype(jnp.float32)
        logits = jnp.sum(pooled * features, axis=1) * inv_root
        loss_grad = ((jax.nn.sigmoid(logits) - labels[step_no].astype(jnp.float32))[:, None] * features * inv_root).astype(jnp.bfloat16)
        weighted = weights[..., None] * loss_grad.astype(jnp.float32)[:, None, None, :]
        row_grad = jax.ops.segment_sum(weighted.reshape(-1, E), flat_ids.reshape(-1), num_segments=N_SHARD * act_rows)
        current = current - step_rate * row_grad
        logit_list.append(logits)
    return row_index, current - initial, jnp.stack(logit_list)


def reference(emb_table, active_blocks, hit_shards, lookup_slot, lookup_offset, block_weight, dense_feat, labels):
    def visit_group(summed, group_no):
        row_index, row_delta, logits = group_round(emb_table, active_blocks[group_no], hit_shards[group_no], lookup_slot[group_no], lookup_offset[group_no], block_weight[group_no], dense_feat[group_no], labels[group_no])
        return summed.at[row_index].add(row_delta), logits

    start = jnp.zeros((N_SHARD * ROWS_DEV, E), jnp.float32)
    summed, step_logits = lax.scan(visit_group, start, jnp.arange(N_REPLICA, dtype=jnp.int32))
    new_table = emb_table + summed / N_REPLICA
    return (new_table, step_logits)
```

```python
import functools

import jax
import jax.numpy as jnp
from jax import lax
from jax.experimental import pallas as pl
from jax.experimental.pallas import tpu as pltpu
from jax.sharding import Mesh
from jax.sharding import PartitionSpec as P

BLK = 16
STRIDE = 16
META = 12
step_rate = 1.0

GROUP = ("x", "b", "c", "y")
HOME = ("a", "b", "c", "h")


def split3(v):
    hi = v.astype(jnp.bfloat16)
    rest = v - hi.astype(jnp.float32)
    mid = rest.astype(jnp.bfloat16)
    return hi, mid, (rest - mid.astype(jnp.float32)).astype(jnp.bfloat16)


def dot(lhs, rhs, contract=((1,), (0,))):
    return lax.dot_general(lhs, rhs, (contract, ((), ())), preferred_element_type=jnp.float32)


def iota(shape, axis):
    return lax.broadcasted_iota(jnp.int32, shape, axis)


def pack_kernel(shards, meta_ref, feat_ref, out_ref, slot_ref):
    meta = meta_ref[0].astype(jnp.float32)
    samples = meta.shape[1]
    hits = 2 * samples

    def pair(first, second):
        return jnp.concatenate([meta[first : first + 1], meta[second : second + 1]], axis=1)

    target = pair(0, 1).astype(jnp.int32)
    chosen = iota((shards, hits), 0) == target
    onehot = chosen.astype(jnp.float32).astype(jnp.bfloat16)
    before = (iota((hits, hits), 0) < iota((hits, hits), 1)).astype(jnp.float32).astype(jnp.bfloat16)
    rank = jnp.sum(jnp.where(chosen, dot(onehot, before), 0.0), axis=0, keepdims=True)
    rank_i = rank.astype(jnp.int32)
    slot = target * STRIDE + rank_i
    place = (iota((shards * STRIDE, hits), 0) == slot).astype(jnp.float32).astype(jnp.bfloat16)
    feats = feat_ref[0]
    packed = dot(place, jnp.concatenate([feats, feats], axis=0))
    other = jnp.concatenate([rank[:, samples:], rank[:, :samples]], axis=1)
    values = [pair(2 + n, 6 + n) for n in range(4)] + [pair(1, 0), other, pair(10, 10), jnp.ones_like(rank)]
    lane_of = iota((STRIDE, hits), 0) == rank_i
    spread = jnp.concatenate([jnp.where(lane_of, value, 0.0) for value in values], axis=0)
    rows = dot(onehot, spread.astype(jnp.bfloat16), ((1,), (1,)))
    at_row = iota((shards * STRIDE, shards), 0) == iota((shards * STRIDE, shards), 1) * STRIDE + META
    packed = packed + dot(at_row.astype(jnp.float32).astype(jnp.bfloat16), rows.astype(jnp.bfloat16))
    out_ref[...] = packed.astype(jnp.bfloat16).reshape(out_ref.shape)
    slot_ref[0] = slot


def pack(meta, feats, shards):
    steps, samples, width = feats.shape
    return pl.pallas_call(
        functools.partial(pack_kernel, shards),
        grid=(steps,),
        in_specs=[
            pl.BlockSpec((1, 16, samples), lambda t: (t, 0, 0)),
            pl.BlockSpec((1, samples, width), lambda t: (t, 0, 0)),
        ],
        out_specs=[
            pl.BlockSpec((shards, 1, STRIDE, width), lambda t: (0, t, 0, 0)),
            pl.BlockSpec((1, 1, 2 * samples), lambda t: (t, 0, 0)),
        ],
        out_shape=[
            jax.ShapeDtypeStruct((shards, steps, STRIDE, width), jnp.bfloat16),
            jax.ShapeDtypeStruct((steps, 1, 2 * samples), jnp.int32),
        ],
        compiler_params=pltpu.CompilerParams(vmem_limit_bytes=40 << 20),
    )(meta, feats)


def prep_kernel(act_rows, got_ref, counts_ref, cols_ref):
    shards, _, _, width = got_ref.shape
    slots = shards * STRIDE
    tiles = got_ref[...].reshape(shards, STRIDE, width).astype(jnp.float32)
    meta = jnp.broadcast_to(tiles[:, META : META + 1, :], tiles.shape).reshape(slots, width)
    own = iota((slots, width), 1) % STRIDE == iota((slots, width), 0) % STRIDE
    fold = iota((width, width), 0) // STRIDE == iota((width, width), 1)
    cols = dot(
        jnp.where(own, meta, 0.0).astype(jnp.bfloat16),
        fold.astype(jnp.float32).astype(jnp.bfloat16),
    )
    cols_ref[...] = cols.astype(jnp.bfloat16)
    row_no = (iota((slots, act_rows), 1) + 1).astype(jnp.float32)
    counts = jnp.zeros((slots, act_rows), jnp.float32)
    for n in range(4):
        counts = counts + jnp.where(row_no == cols[:, n : n + 1], 1.0, 0.0)
    counts_ref[...] = counts.astype(jnp.bfloat16)


def prep(got, step_no, act_rows):
    shards, _, _, width = got.shape
    slots = shards * STRIDE
    return pl.pallas_call(
        functools.partial(prep_kernel, act_rows),
        grid=(1,),
        in_specs=[pl.BlockSpec((shards, 1, STRIDE, width), lambda i: (0, step_no, 0, 0))],
        out_specs=[
            pl.BlockSpec((slots, act_rows), lambda i: (0, 0)),
            pl.BlockSpec((slots, width), lambda i: (0, 0)),
        ],
        out_shape=[
            jax.ShapeDtypeStruct((slots, act_rows), jnp.bfloat16),
            jax.ShapeDtypeStruct((slots, width), jnp.bfloat16),
        ],
        compiler_params=pltpu.CompilerParams(vmem_limit_bytes=40 << 20),
    )(got)


def weight_column(weights_ref, step_no, act_rows):
    row = weights_ref[step_no : step_no + 1, :]
    shape = (act_rows, row.shape[1])
    here = iota(shape, 1) == iota(shape, 0) // BLK
    return jnp.sum(jnp.where(here, row, 0.0), axis=1, keepdims=True)


def forward(weighted, counts, feats, mine_ref):
    width = weighted.shape[1]
    products = sum(dot(counts, part) for part in split3(weighted)) * feats.astype(jnp.float32)
    same = iota((128, 128), 0) == iota((128, 128), 1)
    for k in range(mine_ref.shape[0]):
        column = jnp.sum(products[k * 128 : (k + 1) * 128], axis=1, keepdims=True) * width**-0.5
        mine_ref[k : k + 1, :] = jnp.sum(jnp.where(same, column, 0.0), axis=0, keepdims=True)


def first_kernel(weights_ref, rows_ref, counts_ref, got_ref, mine_ref):
    act_rows, width = rows_ref.shape
    weighted = weight_column(weights_ref, 0, act_rows) * rows_ref[...]
    forward(weighted, counts_ref[...], got_ref[...].reshape(-1, width), mine_ref)


def gradient(table_ref, mine_ref, cols_ref, got_ref, counts_ref, grad_ref):
    shards, blocks, _ = table_ref.shape
    width = got_ref.shape[3]
    feats = got_ref[...].reshape(-1, width)
    row, lane = iota((128, 128), 0), iota((128, 128), 1)
    for k in range(blocks):
        cols = cols_ref[k * 128 : (k + 1) * 128, :].astype(jnp.float32)
        wanted = iota((128, shards), 1).astype(jnp.float32) == cols[:, 4:5]
        wanted = wanted.astype(jnp.float32).astype(jnp.bfloat16)
        found = sum(dot(wanted, part) for part in split3(table_ref[:, k, :]))
        at = (row // STRIDE) * STRIDE + cols[:, 5:6].astype(jnp.int32)
        partner = jnp.sum(jnp.where(lane == at, found, 0.0), axis=1, keepdims=True)
        own = jnp.sum(jnp.where(lane == row, mine_ref[k : k + 1, :], 0.0), axis=1, keepdims=True)
        error = jax.nn.sigmoid(own + partner) - cols[:, 6:7]
        part = error * feats[k * 128 : (k + 1) * 128].astype(jnp.float32) * width**-0.5
        grad_ref[k * 128 : (k + 1) * 128, :] = part.astype(jnp.bfloat16)
    return dot(counts_ref[...], grad_ref[...], ((0,), (0,)))


def step_kernel(
    step_no, weights_ref, rows_ref, table_ref, mine_ref, cols_ref, got_ref, counts_ref,
    next_got_ref, next_counts_ref, new_rows_ref, new_mine_ref, grad_ref,
):
    act_rows, width = rows_ref.shape
    row_grad = gradient(table_ref, mine_ref, cols_ref, got_ref, counts_ref, grad_ref)
    rows = rows_ref[...] - step_rate * (weight_column(weights_ref, step_no, act_rows) * row_grad)
    new_rows_ref[...] = rows
    weighted = weight_column(weights_ref, step_no + 1, act_rows) * rows
    forward(weighted, next_counts_ref[...], next_got_ref[...].reshape(-1, width), new_mine_ref)


def last_kernel(
    step_no, weights_ref, rows_ref, initial_ref, table_ref, mine_ref, cols_ref, got_ref, counts_ref,
    delta_ref, grad_ref,
):
    act_rows = rows_ref.shape[0]
    row_grad = gradient(table_ref, mine_ref, cols_ref, got_ref, counts_ref, grad_ref)
    rows = rows_ref[...] - step_rate * (weight_column(weights_ref, step_no, act_rows) * row_grad)
    delta_ref[...] = (rows - initial_ref[...]).astype(jnp.bfloat16)


def call(kernel, args, outs, scratch=()):
    specs, arrays = [], []
    for arg in args:
        if isinstance(arg, tuple):
            array, step_no = arg
            block = (array.shape[0], 1) + array.shape[2:]
            specs.append(pl.BlockSpec(block, functools.partial(lambda s, i: (0, s, 0, 0), step_no)))
            arrays.append(array)
        else:
            specs.append(pl.BlockSpec(arg.shape, functools.partial(lambda n, i: (0,) * n, arg.ndim)))
            arrays.append(arg)
    out_specs = [
        pl.BlockSpec(out.shape, functools.partial(lambda n, i: (0,) * n, len(out.shape))) for out in outs
    ]
    result = pl.pallas_call(
        kernel,
        grid=(1,),
        in_specs=specs,
        out_specs=out_specs,
        out_shape=list(outs),
        scratch_shapes=list(scratch),
        compiler_params=pltpu.CompilerParams(vmem_limit_bytes=40 << 20),
    )(*arrays)
    return result


def merge_kernel(blocks_ref, core_ref, table_ref, mine_ref, other_ref, out_ref):
    places, act_rows, _ = mine_ref.shape
    active = act_rows // BLK
    groups = 2 * places
    low = core_ref[0] == 0
    out_ref[...] = table_ref[...]

    def one(n, carry):
        place, slot = n // active, n % active
        at = pl.ds(pl.multiple_of(slot * BLK, BLK), BLK)
        mine = mine_ref[place, at, :].astype(jnp.float32)
        other = other_ref[place, at, :].astype(jnp.float32)
        for c, value in enumerate((jnp.where(low, mine, other), jnp.where(low, other, mine))):
            where = pl.ds(pl.multiple_of(blocks_ref[2 * place + c, slot] * BLK, BLK), BLK)
            out_ref[where, :] = out_ref[where, :] + value * (1.0 / groups)
        return carry

    lax.fori_loop(0, places * active, one, 0, unroll=4)


def merge(blocks, core, table, mine, other):
    smem = pl.BlockSpec(memory_space=pltpu.SMEM)
    vmem = pl.BlockSpec(memory_space=pltpu.VMEM)
    return pl.pallas_call(
        merge_kernel,
        in_specs=[smem, smem, vmem, vmem, vmem],
        out_specs=vmem,
        out_shape=jax.ShapeDtypeStruct(table.shape, jnp.float32),
        compiler_params=pltpu.CompilerParams(vmem_limit_bytes=40 << 20),
    )(blocks, core, table, mine, other)


def body(turn, sizes, emb_table, active_blocks, hit_shards, lookup_slot, lookup_offset, block_weight, dense_feat, labels):
    shards = sizes["x"] * sizes["h"] * sizes["y"]
    _, steps, samples, _ = hit_shards.shape
    width = emb_table.shape[1]
    active = active_blocks.shape[2]
    act_rows = active * BLK
    slots = shards * STRIDE
    within = jnp.arange(BLK, dtype=jnp.int32)

    there = functools.partial(lax.ppermute, axis_name=HOME, perm=turn)
    looked = (lookup_slot[0] * BLK + lookup_offset[0] + 1).transpose(0, 2, 3, 1).reshape(steps, 8, samples)
    meta = jnp.concatenate(
        [
            hit_shards[0].transpose(0, 2, 1),
            looked,
            labels[0][:, None, :],
            jnp.zeros((steps, 5, samples), jnp.int32),
        ],
        axis=1,
    ).astype(jnp.bfloat16)
    meta = there(meta)
    feats = there(dense_feat[0])
    my_blocks = active_blocks[lax.axis_index(("a", "b", "c")), 0]
    local_index = (my_blocks[:, None] * BLK + within[None, :]).reshape(-1)
    weights = jnp.pad(block_weight[0, :, 0], ((0, 8 - steps), (0, width - active)))
    carried = there(jnp.concatenate([emb_table[local_index], weights], axis=0))
    initial, weights = carried[:act_rows], carried[act_rows:]

    packed, slot_of = pack(meta, feats, shards)
    got = lax.all_to_all(packed, GROUP, 0, 0, tiled=True)

    rows_like = jax.ShapeDtypeStruct((act_rows, width), jnp.float32)
    mine_like = jax.ShapeDtypeStruct((slots // 128, 128), jnp.float32)
    delta_like = jax.ShapeDtypeStruct((act_rows, width), jnp.bfloat16)
    scratch = [pltpu.VMEM((slots, width), jnp.bfloat16)]
    prepared = [prep(got, t, act_rows) for t in range(steps)]
    rows = initial
    (mine,) = call(first_kernel, [weights, rows, prepared[0][0], (got, 0)], [mine_like])
    tables = []
    for t in range(steps):
        table = lax.all_to_all(jnp.broadcast_to(mine[None], (shards,) + mine.shape), GROUP, 0, 0, tiled=True)
        tables.append(table)
        counts, cols = prepared[t]
        if t + 1 < steps:
            rows, mine = call(
                functools.partial(step_kernel, t),
                [weights, rows, table, mine, cols, (got, t), counts, (got, t + 1), prepared[t + 1][0]],
                [rows_like, mine_like],
                scratch,
            )
        else:
            (delta,) = call(
                functools.partial(last_kernel, t),
                [weights, rows, initial, table, mine, cols, (got, t), counts],
                [delta_like],
                scratch,
            )

    delta = there(delta)
    mine = lax.all_to_all(jnp.broadcast_to(delta[None], (sizes["a"] * 2,) + delta.shape), ("a", "b"), 0, 0, tiled=True)
    other = lax.ppermute(mine, "c", [(0, 1), (1, 0)])
    new_table = merge(active_blocks[:, 0], lax.axis_index("c")[None], emb_table, mine, other)

    me = lax.axis_index(GROUP)
    held = jnp.stack([lax.dynamic_slice(table.reshape(shards, slots), (0, me * STRIDE), (shards, STRIDE)) for table in tables])
    slot_of = slot_of.reshape(steps, 1, 2 * samples)
    onehot = (jnp.arange(shards)[None, :, None] == slot_of // STRIDE).astype(jnp.float32)
    picked = jnp.einsum("tsj,tsi->tji", held, onehot, precision=lax.Precision.HIGHEST)
    picked = jnp.sum(jnp.where(jnp.arange(STRIDE)[None, :, None] == slot_of % STRIDE, picked, 0.0), axis=1)
    logits = there(picked[:, :samples] + picked[:, samples:])
    return new_table, logits[None]


def solution(mesh):
    shards = mesh.shape["shard"]
    y = min(4, shards // 4)
    sizes = {"a": mesh.shape["replica"] // 4, "b": 2, "c": 2, "x": shards // 4 // y, "h": 4, "y": y}
    finer = Mesh(mesh.devices.reshape(tuple(sizes.values())), tuple(sizes))
    index = lambda a, b, c, h: ((a * 2 + b) * 2 + c) * 4 + h
    turn = [
        (index(a, b, c, h), index((a + sizes["a"] // 2) % sizes["a"], h // 2, h % 2, b * 2 + c))
        for a in range(sizes["a"])
        for b in range(2)
        for c in range(2)
        for h in range(4)
    ]
    group, shard = ("a", "b", "c"), ("x", "h", "y")
    placed = (
        P(shard, None),
        P(None, shard, None),
        P(group, None, shard, None),
        P(group, None, shard, None, None),
        P(group, None, shard, None, None),
        P(group, None, shard, None),
        P(group, None, shard, None),
        P(group, None, shard),
    )
    return jax.shard_map(
        functools.partial(body, turn, sizes),
        mesh=finer,
        in_specs=placed,
        out_specs=(P(shard, None), P(group, None, shard)),
        check_vma=False,
    )
```

```python
import functools

import jax
import jax.numpy as jnp
from jax import lax
from jax.experimental import pallas as pl
from jax.experimental.pallas import tpu as pltpu
from jax.sharding import Mesh
from jax.sharding import PartitionSpec as P

BLK = 16
STRIDE = 16
META = 12
VMEM_LIMIT = 16 << 20
step_rate = 1.0

GROUP = ("x", "b", "c", "y")
HOME = ("a", "b", "c", "h")


def split3(v):
    hi = v.astype(jnp.bfloat16)
    rest = v - hi.astype(jnp.float32)
    mid = rest.astype(jnp.bfloat16)
    return hi, mid, (rest - mid.astype(jnp.float32)).astype(jnp.bfloat16)


def dot(lhs, rhs, contract=((1,), (0,))):
    return lax.dot_general(lhs, rhs, (contract, ((), ())), preferred_element_type=jnp.float32)


def iota(shape, axis):
    return lax.broadcasted_iota(jnp.int32, shape, axis)


def pack_kernel(shards, meta_ref, feat_ref, out_ref, slot_ref):
    meta = meta_ref[0].astype(jnp.float32)
    samples = meta.shape[1]
    hits = 2 * samples

    def pair(first, second):
        return jnp.concatenate([meta[first : first + 1], meta[second : second + 1]], axis=1)

    target = pair(0, 1).astype(jnp.int32)
    chosen = iota((shards, hits), 0) == target
    onehot = chosen.astype(jnp.float32).astype(jnp.bfloat16)
    before = (iota((hits, hits), 0) < iota((hits, hits), 1)).astype(jnp.float32).astype(jnp.bfloat16)
    rank = jnp.sum(jnp.where(chosen, dot(onehot, before), 0.0), axis=0, keepdims=True)
    rank_i = rank.astype(jnp.int32)
    slot = target * STRIDE + rank_i
    place = (iota((shards * STRIDE, hits), 0) == slot).astype(jnp.float32).astype(jnp.bfloat16)
    feats = feat_ref[0]
    packed = dot(place, jnp.concatenate([feats, feats], axis=0))
    other = jnp.concatenate([rank[:, samples:], rank[:, :samples]], axis=1)
    values = [pair(2 + n, 6 + n) for n in range(4)] + [pair(1, 0), other, pair(10, 10), jnp.ones_like(rank)]
    lane_of = iota((STRIDE, hits), 0) == rank_i
    spread = jnp.concatenate([jnp.where(lane_of, value, 0.0) for value in values], axis=0)
    rows = dot(onehot, spread.astype(jnp.bfloat16), ((1,), (1,)))
    at_row = iota((shards * STRIDE, shards), 0) == iota((shards * STRIDE, shards), 1) * STRIDE + META
    packed = packed + dot(at_row.astype(jnp.float32).astype(jnp.bfloat16), rows.astype(jnp.bfloat16))
    out_ref[...] = packed.astype(jnp.bfloat16).reshape(out_ref.shape)
    slot_ref[0] = slot


def pack(meta, feats, shards):
    steps, samples, width = feats.shape
    return pl.pallas_call(
        functools.partial(pack_kernel, shards),
        grid=(steps,),
        in_specs=[
            pl.BlockSpec((1, 16, samples), lambda t: (t, 0, 0)),
            pl.BlockSpec((1, samples, width), lambda t: (t, 0, 0)),
        ],
        out_specs=[
            pl.BlockSpec((shards, 1, STRIDE, width), lambda t: (0, t, 0, 0)),
            pl.BlockSpec((1, 1, 2 * samples), lambda t: (t, 0, 0)),
        ],
        out_shape=[
            jax.ShapeDtypeStruct((shards, steps, STRIDE, width), jnp.bfloat16),
            jax.ShapeDtypeStruct((steps, 1, 2 * samples), jnp.int32),
        ],
        compiler_params=pltpu.CompilerParams(vmem_limit_bytes=VMEM_LIMIT),
    )(meta, feats)


def prep_kernel(act_rows, got_ref, counts_ref, cols_ref):
    shards, _, _, width = got_ref.shape
    slots = shards * STRIDE
    tiles = got_ref[...].reshape(shards, STRIDE, width).astype(jnp.float32)
    meta = jnp.broadcast_to(tiles[:, META : META + 1, :], tiles.shape).reshape(slots, width)
    own = iota((slots, width), 1) % STRIDE == iota((slots, width), 0) % STRIDE
    fold = iota((width, width), 0) // STRIDE == iota((width, width), 1)
    cols = dot(
        jnp.where(own, meta, 0.0).astype(jnp.bfloat16),
        fold.astype(jnp.float32).astype(jnp.bfloat16),
    )
    cols_ref[...] = cols.astype(jnp.bfloat16)
    row_no = (iota((slots, act_rows), 1) + 1).astype(jnp.float32)
    counts = jnp.zeros((slots, act_rows), jnp.float32)
    for n in range(4):
        counts = counts + jnp.where(row_no == cols[:, n : n + 1], 1.0, 0.0)
    counts_ref[...] = counts.astype(jnp.bfloat16)


def prep(got, step_no, act_rows):
    shards, _, _, width = got.shape
    slots = shards * STRIDE
    return pl.pallas_call(
        functools.partial(prep_kernel, act_rows),
        grid=(1,),
        in_specs=[pl.BlockSpec((shards, 1, STRIDE, width), lambda i: (0, step_no, 0, 0))],
        out_specs=[
            pl.BlockSpec((slots, act_rows), lambda i: (0, 0)),
            pl.BlockSpec((slots, width), lambda i: (0, 0)),
        ],
        out_shape=[
            jax.ShapeDtypeStruct((slots, act_rows), jnp.bfloat16),
            jax.ShapeDtypeStruct((slots, width), jnp.bfloat16),
        ],
        compiler_params=pltpu.CompilerParams(vmem_limit_bytes=VMEM_LIMIT),
    )(got)


def weight_column(weights_ref, step_no, act_rows):
    row = weights_ref[step_no : step_no + 1, :]
    shape = (act_rows, row.shape[1])
    here = iota(shape, 1) == iota(shape, 0) // BLK
    return jnp.sum(jnp.where(here, row, 0.0), axis=1, keepdims=True)


def forward(weighted, counts, feats, mine_ref):
    width = weighted.shape[1]
    products = sum(dot(counts, part) for part in split3(weighted)) * feats.astype(jnp.float32)
    same = iota((128, 128), 0) == iota((128, 128), 1)
    mine = []
    for k in range(mine_ref.shape[1]):
        column = jnp.sum(products[k * 128 : (k + 1) * 128], axis=1, keepdims=True) * width**-0.5
        mine.append(jnp.sum(jnp.where(same, column, 0.0), axis=0, keepdims=True))
    mine = jnp.concatenate(mine, axis=0)
    mine_ref[...] = jnp.broadcast_to(mine[None], mine_ref.shape)


def first_kernel(weights_ref, rows_ref, counts_ref, got_ref, mine_ref):
    act_rows, width = rows_ref.shape
    weighted = weight_column(weights_ref, 0, act_rows) * rows_ref[...]
    forward(weighted, counts_ref[...], got_ref[...].reshape(-1, width), mine_ref)


def gradient(table_ref, mine_ref, cols_ref, got_ref, counts_ref, grad_ref):
    shards, blocks, _ = table_ref.shape
    width = got_ref.shape[3]
    feats = got_ref[...].reshape(-1, width)
    row, lane = iota((128, 128), 0), iota((128, 128), 1)
    for k in range(blocks):
        cols = cols_ref[k * 128 : (k + 1) * 128, :].astype(jnp.float32)
        wanted = iota((128, shards), 1).astype(jnp.float32) == cols[:, 4:5]
        wanted = wanted.astype(jnp.float32).astype(jnp.bfloat16)
        found = sum(dot(wanted, part) for part in split3(table_ref[:, k, :]))
        at = (row // STRIDE) * STRIDE + cols[:, 5:6].astype(jnp.int32)
        partner = jnp.sum(jnp.where(lane == at, found, 0.0), axis=1, keepdims=True)
        own = jnp.sum(jnp.where(lane == row, mine_ref[0, k : k + 1, :], 0.0), axis=1, keepdims=True)
        error = jax.nn.sigmoid(own + partner) - cols[:, 6:7]
        part = error * feats[k * 128 : (k + 1) * 128].astype(jnp.float32) * width**-0.5
        grad_ref[k * 128 : (k + 1) * 128, :] = part.astype(jnp.bfloat16)
    return dot(counts_ref[...], grad_ref[...], ((0,), (0,)))


def step_kernel(
    step_no, weights_ref, rows_ref, table_ref, mine_ref, cols_ref, got_ref, counts_ref,
    next_got_ref, next_counts_ref, new_rows_ref, new_mine_ref, grad_ref,
):
    act_rows, width = rows_ref.shape
    row_grad = gradient(table_ref, mine_ref, cols_ref, got_ref, counts_ref, grad_ref)
    rows = rows_ref[...] - step_rate * (weight_column(weights_ref, step_no, act_rows) * row_grad)
    new_rows_ref[...] = rows
    weighted = weight_column(weights_ref, step_no + 1, act_rows) * rows
    forward(weighted, next_counts_ref[...], next_got_ref[...].reshape(-1, width), new_mine_ref)


def own_logits(me, table_ref, slot):
    shards, blocks, _ = table_ref.shape
    hits = slot.shape[1]
    part = sum(jnp.where(me // (128 // STRIDE) == k, table_ref[:, k, :], 0.0) for k in range(blocks))
    onehot = iota((shards, hits), 0) == slot // STRIDE
    onehot = onehot.astype(jnp.float32).astype(jnp.bfloat16)
    found = sum(dot(term, onehot, ((0,), (0,))) for term in split3(part))
    at = (me % (128 // STRIDE)) * STRIDE + slot % STRIDE
    picked = jnp.sum(jnp.where(iota((128, hits), 0) == at, found, 0.0), axis=0, keepdims=True)
    logits = picked[:, : hits // 2] + picked[:, hits // 2 :]
    return jnp.concatenate([logits[:, n : n + 128] for n in range(0, hits // 2, 128)], axis=0)


def early_kernel(me_ref, slot_ref, *refs):
    tables, out_ref = refs[:-1], refs[-1]
    done = [own_logits(me_ref[0], table_ref, slot_ref[t]) for t, table_ref in enumerate(tables)]
    missing = out_ref.shape[0] - sum(part.shape[0] for part in done)
    out_ref[...] = jnp.concatenate(done + [jnp.zeros((missing, 128), jnp.float32)], axis=0)


def last_kernel(
    step_no, me_ref, slot_ref, early_ref, weights_ref, rows_ref, initial_ref, table_ref, mine_ref, cols_ref, got_ref,
    counts_ref, back_ref, grad_ref,
):
    act_rows = rows_ref.shape[0]
    row_grad = gradient(table_ref, mine_ref, cols_ref, got_ref, counts_ref, grad_ref)
    rows = rows_ref[...] - step_rate * (weight_column(weights_ref, step_no, act_rows) * row_grad)
    back_ref[:act_rows, :] = (rows - initial_ref[...]).astype(jnp.bfloat16)
    logits = own_logits(me_ref[0], table_ref, slot_ref[step_no])
    known = early_ref.shape[0] - logits.shape[0]
    logits = jnp.concatenate([early_ref[:known, :], logits], axis=0)
    terms = [term.astype(jnp.float32) for term in split3(logits)]
    back_ref[act_rows:, :] = jnp.concatenate(terms + [jnp.zeros_like(logits)], axis=0).astype(jnp.bfloat16)


def call(kernel, args, outs, scratch=()):
    specs, arrays = [], []
    for arg in args:
        if isinstance(arg, tuple):
            array, step_no = arg
            block = (array.shape[0], 1) + array.shape[2:]
            specs.append(pl.BlockSpec(block, functools.partial(lambda s, i: (0, s, 0, 0), step_no)))
            arrays.append(array)
        elif arg.size == 1:
            specs.append(pl.BlockSpec(memory_space=pltpu.SMEM))
            arrays.append(arg)
        else:
            specs.append(pl.BlockSpec(arg.shape, functools.partial(lambda n, i: (0,) * n, arg.ndim)))
            arrays.append(arg)
    out_specs = [
        pl.BlockSpec(out.shape, functools.partial(lambda n, i: (0,) * n, len(out.shape))) for out in outs
    ]
    result = pl.pallas_call(
        kernel,
        grid=(1,),
        in_specs=specs,
        out_specs=out_specs,
        out_shape=list(outs),
        scratch_shapes=list(scratch),
        compiler_params=pltpu.CompilerParams(vmem_limit_bytes=VMEM_LIMIT),
    )(*arrays)
    return result


def merge_kernel(blocks_ref, core_ref, table_ref, mine_ref, other_ref, out_ref):
    places, act_rows, _ = mine_ref.shape
    active = act_rows // BLK
    groups = 2 * places
    low = core_ref[0] == 0
    out_ref[...] = table_ref[...]

    def one(n, carry):
        place, slot = n // active, n % active
        at = pl.ds(pl.multiple_of(slot * BLK, BLK), BLK)
        mine = mine_ref[place, at, :].astype(jnp.float32)
        other = other_ref[place, at, :].astype(jnp.float32)
        for c, value in enumerate((jnp.where(low, mine, other), jnp.where(low, other, mine))):
            where = pl.ds(pl.multiple_of(blocks_ref[2 * place + c, slot] * BLK, BLK), BLK)
            out_ref[where, :] = out_ref[where, :] + value * (1.0 / groups)
        return carry

    lax.fori_loop(0, places * active, one, 0, unroll=4)


def merge(blocks, core, table, mine, other):
    smem = pl.BlockSpec(memory_space=pltpu.SMEM)
    vmem = pl.BlockSpec(memory_space=pltpu.VMEM)
    return pl.pallas_call(
        merge_kernel,
        in_specs=[smem, smem, vmem, vmem, vmem],
        out_specs=vmem,
        out_shape=jax.ShapeDtypeStruct(table.shape, jnp.float32),
        compiler_params=pltpu.CompilerParams(vmem_limit_bytes=VMEM_LIMIT),
    )(blocks, core, table, mine, other)


def body(turn, sizes, emb_table, active_blocks, hit_shards, lookup_slot, lookup_offset, block_weight, dense_feat, labels):
    shards = sizes["x"] * sizes["h"] * sizes["y"]
    _, steps, samples, _ = hit_shards.shape
    width = emb_table.shape[1]
    active = active_blocks.shape[2]
    act_rows = active * BLK
    slots = shards * STRIDE
    within = jnp.arange(BLK, dtype=jnp.int32)

    there = functools.partial(lax.ppermute, axis_name=HOME, perm=turn)
    looked = (lookup_slot[0] * BLK + lookup_offset[0] + 1).transpose(0, 2, 3, 1).reshape(steps, 8, samples)
    meta = jnp.concatenate(
        [
            hit_shards[0].transpose(0, 2, 1),
            looked,
            labels[0][:, None, :],
            jnp.zeros((steps, 5, samples), jnp.int32),
        ],
        axis=1,
    ).astype(jnp.bfloat16)
    meta = there(meta)
    feats = there(dense_feat[0])
    my_blocks = active_blocks[lax.axis_index(("a", "b", "c")), 0]
    local_index = (my_blocks[:, None] * BLK + within[None, :]).reshape(-1)
    weights = jnp.pad(block_weight[0, :, 0], ((0, 8 - steps), (0, width - active)))
    carried = there(jnp.concatenate([emb_table[local_index], weights], axis=0))
    meta, feats, carried = lax.optimization_barrier((meta, feats, carried))
    initial, weights = carried[:act_rows], carried[act_rows:]

    packed, slot_of = pack(meta, feats, shards)
    got = lax.all_to_all(packed, GROUP, 0, 0, tiled=True)

    logit_rows = steps * samples // 128
    rows_like = jax.ShapeDtypeStruct((act_rows, width), jnp.float32)
    mine_like = jax.ShapeDtypeStruct((shards, slots // 128, 128), jnp.float32)
    early_like = jax.ShapeDtypeStruct((logit_rows, 128), jnp.float32)
    back_like = jax.ShapeDtypeStruct((act_rows + 4 * logit_rows, width), jnp.bfloat16)
    scratch = [pltpu.VMEM((slots, width), jnp.bfloat16)]
    me = lax.axis_index(GROUP)[None]
    prepared = [prep(got, t, act_rows) for t in range(steps)]
    rows = initial
    (mine,) = call(first_kernel, [weights, rows, prepared[0][0], (got, 0)], [mine_like])
    tables = []
    for t in range(steps):
        table = lax.all_to_all(mine, GROUP, 0, 0, tiled=True)
        counts, cols = prepared[t]
        if t + 1 < steps:
            rows, mine = call(
                functools.partial(step_kernel, t),
                [weights, rows, table, mine, cols, (got, t), counts, (got, t + 1), prepared[t + 1][0]],
                [rows_like, mine_like],
                scratch,
            )
            tables.append(table)
        else:
            (early,) = call(early_kernel, [me, slot_of, *tables], [early_like])
            (back,) = call(
                functools.partial(last_kernel, t),
                [me, slot_of, early, weights, rows, initial, table, mine, cols, (got, t), counts],
                [back_like],
                scratch,
            )

    back = there(back)
    delta, terms = back[:act_rows], back[act_rows:].astype(jnp.float32).reshape(4, logit_rows, 128)
    mine = lax.all_to_all(jnp.broadcast_to(delta[None], (sizes["a"] * 2,) + delta.shape), ("a", "b"), 0, 0, tiled=True)
    other = lax.ppermute(mine, "c", [(0, 1), (1, 0)])
    new_table = merge(active_blocks[:, 0], lax.axis_index("c")[None], emb_table, mine, other)
    logits = (terms[0] + terms[1] + terms[2]).reshape(steps, samples)
    return new_table, logits[None]


def solution(mesh):
    shards = mesh.shape["shard"]
    y = min(4, shards // 4)
    sizes = {"a": mesh.shape["replica"] // 4, "b": 2, "c": 2, "x": shards // 4 // y, "h": 4, "y": y}
    finer = Mesh(mesh.devices.reshape(tuple(sizes.values())), tuple(sizes))
    index = lambda a, b, c, h: ((a * 2 + b) * 2 + c) * 4 + h
    turn = [
        (index(a, b, c, h), index((a + sizes["a"] // 2) % sizes["a"], h // 2, h % 2, b * 2 + c))
        for a in range(sizes["a"])
        for b in range(2)
        for c in range(2)
        for h in range(4)
    ]
    group, shard = ("a", "b", "c"), ("x", "h", "y")
    placed = (
        P(shard, None),
        P(None, shard, None),
        P(group, None, shard, None),
        P(group, None, shard, None, None),
        P(group, None, shard, None, None),
        P(group, None, shard, None),
        P(group, None, shard, None),
        P(group, None, shard),
    )
    return jax.shard_map(
        functools.partial(body, turn, sizes),
        mesh=finer,
        in_specs=placed,
        out_specs=(P(shard, None), P(group, None, shard)),
        check_vma=False,
    )
```

```python
import functools

import jax
import jax.numpy as jnp
from jax import lax
from jax.experimental import pallas as pl
from jax.experimental.pallas import tpu as pltpu
from jax.sharding import Mesh
from jax.sharding import PartitionSpec as P

BLK = 16
STRIDE = 16
META = 12
VMEM_LIMIT = 16 << 20
MERGE_LIMIT = 60 << 20
step_rate = 1.0

GROUP = ("x", "b", "c", "y")
HOME = ("a", "b", "c", "h")


def split3(v):
    hi = v.astype(jnp.bfloat16)
    rest = v - hi.astype(jnp.float32)
    mid = rest.astype(jnp.bfloat16)
    return hi, mid, (rest - mid.astype(jnp.float32)).astype(jnp.bfloat16)


def wide(v):
    hi = v.astype(jnp.bfloat16)
    return jnp.concatenate([hi, (v - hi.astype(jnp.float32)).astype(jnp.bfloat16)], axis=1)


def halves(v):
    return v[:, : v.shape[1] // 2] + v[:, v.shape[1] // 2 :]


def dot(lhs, rhs, contract=((1,), (0,))):
    return lax.dot_general(lhs, rhs, (contract, ((), ())), preferred_element_type=jnp.float32)


def iota(shape, axis):
    return lax.broadcasted_iota(jnp.int32, shape, axis)


def pack_kernel(shards, meta_ref, feat_ref, out_ref, slot_ref):
    meta = meta_ref[0].astype(jnp.float32)
    samples = meta.shape[1]
    hits = 2 * samples

    def pair(first, second):
        return jnp.concatenate([meta[first : first + 1], meta[second : second + 1]], axis=1)

    target = pair(0, 1).astype(jnp.int32)
    chosen = iota((shards, hits), 0) == target
    onehot = chosen.astype(jnp.float32).astype(jnp.bfloat16)
    before = (iota((hits, hits), 0) < iota((hits, hits), 1)).astype(jnp.float32).astype(jnp.bfloat16)
    rank = jnp.sum(jnp.where(chosen, dot(onehot, before), 0.0), axis=0, keepdims=True)
    rank_i = rank.astype(jnp.int32)
    slot = target * STRIDE + rank_i
    at = iota((shards * STRIDE, samples), 0)
    place = jnp.where((at == slot[:, :samples]) | (at == slot[:, samples:]), 1.0, 0.0).astype(jnp.bfloat16)
    packed = dot(place, feat_ref[0])
    other = jnp.concatenate([rank[:, samples:], rank[:, :samples]], axis=1)
    values = [pair(2 + n, 6 + n) for n in range(4)] + [pair(1, 0), other, pair(10, 10), jnp.ones_like(rank)]
    lane_of = iota((STRIDE, hits), 0) == rank_i
    spread = jnp.concatenate([jnp.where(lane_of, value, 0.0) for value in values], axis=0)
    rows = dot(onehot, spread.astype(jnp.bfloat16), ((1,), (1,)))
    at_row = iota((shards * STRIDE, shards), 0) == iota((shards * STRIDE, shards), 1) * STRIDE + META
    packed = packed + dot(at_row.astype(jnp.float32).astype(jnp.bfloat16), rows.astype(jnp.bfloat16))
    out_ref[...] = packed.astype(jnp.bfloat16).reshape(out_ref.shape)
    slot_ref[0] = slot


def pack(meta, feats, shards):
    steps, samples, width = feats.shape
    return pl.pallas_call(
        functools.partial(pack_kernel, shards),
        grid=(steps,),
        in_specs=[
            pl.BlockSpec((1, 16, samples), lambda t: (t, 0, 0)),
            pl.BlockSpec((1, samples, width), lambda t: (t, 0, 0)),
        ],
        out_specs=[
            pl.BlockSpec((shards, 1, STRIDE, width), lambda t: (0, t, 0, 0)),
            pl.BlockSpec((1, 1, 2 * samples), lambda t: (t, 0, 0)),
        ],
        out_shape=[
            jax.ShapeDtypeStruct((shards, steps, STRIDE, width), jnp.bfloat16),
            jax.ShapeDtypeStruct((steps, 1, 2 * samples), jnp.int32),
        ],
        compiler_params=pltpu.CompilerParams(vmem_limit_bytes=VMEM_LIMIT),
    )(meta, feats)


def columns(got_ref, step_no):
    tiles = got_ref[:, step_no].astype(jnp.float32)
    width = tiles.shape[2]
    meta = jnp.broadcast_to(tiles[:, META : META + 1, :], tiles.shape).reshape(-1, width)
    own = iota(meta.shape, 1) % STRIDE == iota(meta.shape, 0) % STRIDE
    fold = iota((width, width), 0) // STRIDE == iota((width, width), 1)
    return dot(
        jnp.where(own, meta, 0.0).astype(jnp.bfloat16),
        fold.astype(jnp.float32).astype(jnp.bfloat16),
    )


def lookups(cols, act_rows):
    row_no = (iota((cols.shape[0], act_rows), 1) + 1).astype(jnp.float32)
    return sum(jnp.where(row_no == cols[:, n : n + 1], 1.0, 0.0) for n in range(4))


def own_logits(me, table_ref, slot):
    shards, blocks, _ = table_ref.shape
    hits = slot.shape[1]
    part = sum(jnp.where(me // (128 // STRIDE) == k, table_ref[:, k, :], 0.0) for k in range(blocks))
    onehot = iota((shards, hits), 0) == slot // STRIDE
    onehot = onehot.astype(jnp.float32).astype(jnp.bfloat16)
    found = dot(wide(part), onehot, ((0,), (0,)))
    found = found[:128] + found[128:]
    at = (me % (128 // STRIDE)) * STRIDE + slot % STRIDE
    picked = jnp.sum(jnp.where(iota((128, hits), 0) == at, found, 0.0), axis=0, keepdims=True)
    logits = picked[:, : hits // 2] + picked[:, hits // 2 :]
    return jnp.concatenate([logits[:, n : n + 128] for n in range(0, hits // 2, 128)], axis=0)


def prep_kernel(step_no, steps, me_ref, slot_ref, got_ref, *refs):
    if step_no:
        old_table_ref, *refs = refs
        *refs, logits_ref = refs
        logits_ref[...] = own_logits(me_ref[0], old_table_ref, slot_ref[step_no - 1])
    turned_ref, cols_ref, *next_counts_ref = refs
    act_rows = turned_ref.shape[0]
    cols = columns(got_ref, step_no)
    cols_ref[...] = cols.astype(jnp.bfloat16)
    turned_ref[...] = lookups(cols, act_rows).T.astype(jnp.bfloat16)
    if next_counts_ref:
        next_cols = columns(got_ref, step_no + 1)
        next_counts_ref[0][...] = lookups(next_cols, act_rows).astype(jnp.bfloat16)


def prep(me, slot_of, got, old_table, step_no, act_rows):
    shards, steps, _, width = got.shape
    slots = shards * STRIDE
    outs = [
        jax.ShapeDtypeStruct((act_rows, slots), jnp.bfloat16),
        jax.ShapeDtypeStruct((slots, width), jnp.bfloat16),
    ]
    if step_no + 1 < steps:
        outs.append(jax.ShapeDtypeStruct((slots, act_rows), jnp.bfloat16))
    if step_no:
        outs.append(jax.ShapeDtypeStruct((slot_of.shape[2] // 256, 128), jnp.float32))
    args = [me, slot_of, got] + ([old_table] if step_no else [])
    return call(functools.partial(prep_kernel, step_no, steps), args, outs)


def weight_column(weights_ref, step_no, act_rows):
    row = weights_ref[step_no : step_no + 1, :]
    shape = (act_rows, row.shape[1])
    here = iota(shape, 1) == iota(shape, 0) // BLK
    return jnp.sum(jnp.where(here, row, 0.0), axis=1, keepdims=True)


def forward(weighted, counts, feats, mine_ref):
    width = weighted.shape[1]
    products = halves(dot(counts, wide(weighted))) * feats.astype(jnp.float32)
    same = iota((128, 128), 0) == iota((128, 128), 1)
    mine = []
    for k in range(mine_ref.shape[1]):
        column = jnp.sum(products[k * 128 : (k + 1) * 128], axis=1, keepdims=True) * width**-0.5
        mine.append(jnp.sum(jnp.where(same, column, 0.0), axis=0, keepdims=True))
    mine = jnp.concatenate(mine, axis=0)
    mine_ref[...] = jnp.broadcast_to(mine[None], mine_ref.shape)


def first_kernel(weights_ref, rows_ref, got_ref, mine_ref):
    act_rows, width = rows_ref.shape
    counts = lookups(columns(got_ref, 0), act_rows).astype(jnp.bfloat16)
    weighted = weight_column(weights_ref, 0, act_rows) * rows_ref[...]
    forward(weighted, counts, got_ref[:, 0].reshape(-1, width), mine_ref)


def gradient(step_no, table_ref, mine_ref, cols_ref, got_ref, turned_ref, grad_ref):
    shards, blocks, _ = table_ref.shape
    width = got_ref.shape[3]
    feats = got_ref[:, step_no].reshape(-1, width)
    row, lane = iota((128, 128), 0), iota((128, 128), 1)
    base = (row // STRIDE) * STRIDE
    shard = iota((128, shards), 1).astype(jnp.float32)
    for k in range(blocks):
        cols = cols_ref[k * 128 : (k + 1) * 128, :].astype(jnp.float32)
        wanted = (shard == cols[:, 4:5]).astype(jnp.float32).astype(jnp.bfloat16)
        found = halves(dot(wanted, wide(table_ref[:, k, :])))
        partner = jnp.where(lane == base + cols[:, 5:6].astype(jnp.int32), found, 0.0)
        own = jnp.where(lane == row, mine_ref[0, k : k + 1, :], 0.0)
        error = jax.nn.sigmoid(jnp.sum(partner + own, axis=1, keepdims=True)) - cols[:, 6:7]
        part = error * feats[k * 128 : (k + 1) * 128].astype(jnp.float32) * width**-0.5
        grad_ref[k * 128 : (k + 1) * 128, :] = part.astype(jnp.bfloat16)
    return dot(turned_ref[...], grad_ref[...])


def step_kernel(
    step_no, weights_ref, rows_ref, table_ref, mine_ref, cols_ref, got_ref, turned_ref, next_counts_ref,
    new_rows_ref, new_mine_ref, grad_ref,
):
    act_rows, width = rows_ref.shape
    row_grad = gradient(step_no, table_ref, mine_ref, cols_ref, got_ref, turned_ref, grad_ref)
    rows = rows_ref[...] - step_rate * (weight_column(weights_ref, step_no, act_rows) * row_grad)
    new_rows_ref[...] = rows
    weighted = weight_column(weights_ref, step_no + 1, act_rows) * rows
    forward(weighted, next_counts_ref[...], got_ref[:, step_no + 1].reshape(-1, width), new_mine_ref)


def last_kernel(
    step_no, me_ref, slot_ref, weights_ref, rows_ref, initial_ref, table_ref, mine_ref, cols_ref, got_ref, turned_ref,
    *refs,
):
    *known_refs, back_ref, grad_ref = refs
    act_rows = rows_ref.shape[0]
    row_grad = gradient(step_no, table_ref, mine_ref, cols_ref, got_ref, turned_ref, grad_ref)
    rows = rows_ref[...] - step_rate * (weight_column(weights_ref, step_no, act_rows) * row_grad)
    back_ref[:act_rows, :] = (rows - initial_ref[...]).astype(jnp.bfloat16)
    logits = own_logits(me_ref[0], table_ref, slot_ref[step_no])
    logits = jnp.concatenate([ref[...] for ref in known_refs] + [logits], axis=0)
    terms = [term.astype(jnp.float32) for term in split3(logits)]
    back_ref[act_rows:, :] = jnp.concatenate(terms + [jnp.zeros_like(logits)], axis=0).astype(jnp.bfloat16)


def call(kernel, args, outs, scratch=()):
    smem, vmem = (pl.BlockSpec(memory_space=space) for space in (pltpu.SMEM, pltpu.VMEM))
    return pl.pallas_call(
        kernel,
        in_specs=[smem if arg.size == 1 else vmem for arg in args],
        out_specs=[vmem] * len(outs),
        out_shape=list(outs),
        scratch_shapes=list(scratch),
        compiler_params=pltpu.CompilerParams(vmem_limit_bytes=VMEM_LIMIT),
    )(*args)


def merge_kernel(blocks_ref, core_ref, table_ref, mine_ref, other_ref, out_ref, sem):
    places, act_rows, _ = mine_ref.shape
    active = act_rows // BLK
    groups = 2 * places
    low = core_ref[0] == 0
    copy = pltpu.make_async_copy(table_ref, out_ref, sem)
    copy.start()
    copy.wait()

    def one(place, carry):
        for c in range(2):
            spots, values = [], []
            for slot in range(active):
                at = pl.ds(slot * BLK, BLK)
                mine, other = mine_ref[place, at, :], other_ref[place, at, :]
                value = jnp.where(low, mine, other) if c == 0 else jnp.where(low, other, mine)
                spot = pl.ds(pl.multiple_of(blocks_ref[2 * place + c, slot] * BLK, BLK), BLK)
                spots.append(spot)
                values.append(out_ref[spot, :] + value.astype(jnp.float32) * (1.0 / groups))
            for spot, value in zip(spots, values):
                out_ref[spot, :] = value
        return carry

    lax.fori_loop(0, places, one, 0)


def merge(blocks, core, table, mine, other):
    smem, hbm = (pl.BlockSpec(memory_space=space) for space in (pltpu.SMEM, pltpu.HBM))
    whole = pl.BlockSpec(mine.shape, lambda i: (0, 0, 0))
    return pl.pallas_call(
        merge_kernel,
        grid=(1,),
        in_specs=[smem, smem, hbm, whole, whole],
        out_specs=pl.BlockSpec(table.shape, lambda i: (0, 0)),
        out_shape=jax.ShapeDtypeStruct(table.shape, jnp.float32),
        scratch_shapes=[pltpu.SemaphoreType.DMA],
        compiler_params=pltpu.CompilerParams(vmem_limit_bytes=MERGE_LIMIT),
    )(blocks, core, table, mine, other)


def body(turn, sizes, emb_table, active_blocks, hit_shards, lookup_slot, lookup_offset, block_weight, dense_feat, labels):
    shards = sizes["x"] * sizes["h"] * sizes["y"]
    _, steps, samples, _ = hit_shards.shape
    width = emb_table.shape[1]
    active = active_blocks.shape[2]
    act_rows = active * BLK
    slots = shards * STRIDE
    within = jnp.arange(BLK, dtype=jnp.int32)

    there = functools.partial(lax.ppermute, axis_name=HOME, perm=turn)
    looked = (lookup_slot[0] * BLK + lookup_offset[0] + 1).transpose(0, 2, 3, 1).reshape(steps, 8, samples)
    meta = jnp.concatenate(
        [
            hit_shards[0].transpose(0, 2, 1),
            looked,
            labels[0][:, None, :],
            jnp.zeros((steps, 5, samples), jnp.int32),
        ],
        axis=1,
    ).astype(jnp.bfloat16)
    meta = there(meta)
    feats = there(dense_feat[0])
    my_blocks = active_blocks[lax.axis_index(("a", "b", "c")), 0]
    local_index = (my_blocks[:, None] * BLK + within[None, :]).reshape(-1)
    weights = jnp.pad(block_weight[0, :, 0], ((0, 8 - steps), (0, width - active)))
    carried = there(jnp.concatenate([emb_table[local_index], weights], axis=0))
    meta, feats, carried = lax.optimization_barrier((meta, feats, carried))
    initial, weights = carried[:act_rows], carried[act_rows:]

    packed, slot_of = pack(meta, feats, shards)
    got = lax.all_to_all(packed, GROUP, 0, 0, tiled=True)

    logit_rows = steps * samples // 128
    rows_like = jax.ShapeDtypeStruct((act_rows, width), jnp.float32)
    mine_like = jax.ShapeDtypeStruct((shards, slots // 128, 128), jnp.float32)
    back_like = jax.ShapeDtypeStruct((act_rows + 4 * logit_rows, width), jnp.bfloat16)
    scratch = [pltpu.VMEM((slots, width), jnp.bfloat16)]
    me = lax.axis_index(GROUP)[None]
    rows = initial
    (mine,) = call(first_kernel, [weights, rows, got], [mine_like])
    table, known = None, []
    for t in range(steps):
        turned, cols, *more = prep(me, slot_of, got, table, t, act_rows)
        known += more[1:] if t + 1 < steps else more
        table = lax.all_to_all(mine, GROUP, 0, 0, tiled=True)
        if t + 1 < steps:
            rows, mine = call(
                functools.partial(step_kernel, t),
                [weights, rows, table, mine, cols, got, turned, more[0]],
                [rows_like, mine_like],
                scratch,
            )
        else:
            (back,) = call(
                functools.partial(last_kernel, t),
                [me, slot_of, weights, rows, initial, table, mine, cols, got, turned, *known],
                [back_like],
                scratch,
            )

    back = there(back)
    delta, terms = back[:act_rows], back[act_rows:].astype(jnp.float32).reshape(4, logit_rows, 128)
    mine = lax.all_to_all(jnp.broadcast_to(delta[None], (sizes["a"] * 2,) + delta.shape), ("a", "b"), 0, 0, tiled=True)
    other = lax.ppermute(mine, "c", [(0, 1), (1, 0)])
    new_table = merge(active_blocks[:, 0], lax.axis_index("c")[None], emb_table, mine, other)
    logits = (terms[0] + terms[1] + terms[2]).reshape(steps, samples)
    return new_table, logits[None]


def solution(mesh):
    shards = mesh.shape["shard"]
    y = min(4, shards // 4)
    sizes = {"a": mesh.shape["replica"] // 4, "b": 2, "c": 2, "x": shards // 4 // y, "h": 4, "y": y}
    finer = Mesh(mesh.devices.reshape(tuple(sizes.values())), tuple(sizes))
    index = lambda a, b, c, h: ((a * 2 + b) * 2 + c) * 4 + h
    turn = [
        (index(a, b, c, h), index((a + sizes["a"] // 2) % sizes["a"], h // 2, h % 2, b * 2 + c))
        for a in range(sizes["a"])
        for b in range(2)
        for c in range(2)
        for h in range(4)
    ]
    group, shard = ("a", "b", "c"), ("x", "h", "y")
    placed = (
        P(shard, None),
        P(None, shard, None),
        P(group, None, shard, None),
        P(group, None, shard, None, None),
        P(group, None, shard, None, None),
        P(group, None, shard, None),
        P(group, None, shard, None),
        P(group, None, shard),
    )
    return jax.shard_map(
        functools.partial(body, turn, sizes),
        mesh=finer,
        in_specs=placed,
        out_specs=(P(shard, None), P(group, None, shard)),
        check_vma=False,
    )
```

```python
import functools

import jax
import jax.numpy as jnp
from jax import lax
from jax.experimental import pallas as pl
from jax.experimental.pallas import tpu as pltpu
from jax.sharding import Mesh
from jax.sharding import PartitionSpec as P

BLK = 16
STRIDE = 16
META = 12
VMEM_LIMIT = 16 << 20
MERGE_LIMIT = 60 << 20
COVER = pl.CostEstimate(flops=10**11, bytes_accessed=0, transcendentals=0)
step_rate = 1.0

GROUP = ("x", "b", "c", "y")
HOME = ("a1", "a0", "b", "c", "h")


def split3(v):
    hi = v.astype(jnp.bfloat16)
    rest = v - hi.astype(jnp.float32)
    mid = rest.astype(jnp.bfloat16)
    return hi, mid, (rest - mid.astype(jnp.float32)).astype(jnp.bfloat16)


def wide(v):
    hi = v.astype(jnp.bfloat16)
    return jnp.concatenate([hi, (v - hi.astype(jnp.float32)).astype(jnp.bfloat16)], axis=1)


def halves(v):
    return v[:, : v.shape[1] // 2] + v[:, v.shape[1] // 2 :]


def dot(lhs, rhs, contract=((1,), (0,))):
    return lax.dot_general(lhs, rhs, (contract, ((), ())), preferred_element_type=jnp.float32)


def iota(shape, axis):
    return lax.broadcasted_iota(jnp.int32, shape, axis)


def pack_kernel(shards, meta_ref, feat_ref, out_ref, slot_ref):
    meta = meta_ref[0].astype(jnp.float32)
    samples = meta.shape[1]
    hits = 2 * samples

    def pair(first, second):
        return jnp.concatenate([meta[first : first + 1], meta[second : second + 1]], axis=1)

    target = pair(0, 1).astype(jnp.int32)
    chosen = iota((shards, hits), 0) == target
    onehot = chosen.astype(jnp.float32).astype(jnp.bfloat16)
    before = (iota((hits, hits), 0) < iota((hits, hits), 1)).astype(jnp.float32).astype(jnp.bfloat16)
    rank = jnp.sum(jnp.where(chosen, dot(onehot, before), 0.0), axis=0, keepdims=True)
    rank_i = rank.astype(jnp.int32)
    slot = target * STRIDE + rank_i
    at = iota((shards * STRIDE, samples), 0)
    place = jnp.where((at == slot[:, :samples]) | (at == slot[:, samples:]), 1.0, 0.0).astype(jnp.bfloat16)
    packed = dot(place, feat_ref[0])
    other = jnp.concatenate([rank[:, samples:], rank[:, :samples]], axis=1)
    values = [pair(2 + n, 6 + n) for n in range(4)] + [pair(1, 0), other, pair(10, 10), jnp.ones_like(rank)]
    lane_of = iota((STRIDE, hits), 0) == rank_i
    spread = jnp.concatenate([jnp.where(lane_of, value, 0.0) for value in values], axis=0)
    rows = dot(onehot, spread.astype(jnp.bfloat16), ((1,), (1,)))
    at_row = iota((shards * STRIDE, shards), 0) == iota((shards * STRIDE, shards), 1) * STRIDE + META
    packed = packed + dot(at_row.astype(jnp.float32).astype(jnp.bfloat16), rows.astype(jnp.bfloat16))
    out_ref[...] = packed.astype(jnp.bfloat16).reshape(out_ref.shape)
    slot_ref[0] = slot


def pack(meta, feats, shards):
    steps, samples, width = feats.shape
    return pl.pallas_call(
        functools.partial(pack_kernel, shards),
        grid=(steps,),
        in_specs=[
            pl.BlockSpec((1, 16, samples), lambda t: (t, 0, 0)),
            pl.BlockSpec((1, samples, width), lambda t: (t, 0, 0)),
        ],
        out_specs=[
            pl.BlockSpec((shards, 1, STRIDE, width), lambda t: (0, t, 0, 0)),
            pl.BlockSpec((1, 1, 2 * samples), lambda t: (t, 0, 0)),
        ],
        out_shape=[
            jax.ShapeDtypeStruct((shards, steps, STRIDE, width), jnp.bfloat16),
            jax.ShapeDtypeStruct((steps, 1, 2 * samples), jnp.int32),
        ],
        compiler_params=pltpu.CompilerParams(vmem_limit_bytes=VMEM_LIMIT),
    )(meta, feats)


def columns(got_ref, step_no):
    tiles = got_ref[:, step_no].astype(jnp.float32)
    width = tiles.shape[2]
    meta = jnp.broadcast_to(tiles[:, META : META + 1, :], tiles.shape).reshape(-1, width)
    own = iota(meta.shape, 1) % STRIDE == iota(meta.shape, 0) % STRIDE
    fold = iota((width, width), 0) // STRIDE == iota((width, width), 1)
    return dot(
        jnp.where(own, meta, 0.0).astype(jnp.bfloat16),
        fold.astype(jnp.float32).astype(jnp.bfloat16),
    )


def lookups(cols, act_rows):
    row_no = (iota((cols.shape[0], act_rows), 1) + 1).astype(jnp.float32)
    return sum(jnp.where(row_no == cols[:, n : n + 1], 1.0, 0.0) for n in range(4))


def own_logits(me, table_ref, slot):
    shards, blocks, _ = table_ref.shape
    hits = slot.shape[1]
    part = sum(jnp.where(me // (128 // STRIDE) == k, table_ref[:, k, :], 0.0) for k in range(blocks))
    onehot = iota((shards, hits), 0) == slot // STRIDE
    onehot = onehot.astype(jnp.float32).astype(jnp.bfloat16)
    found = dot(wide(part), onehot, ((0,), (0,)))
    found = found[:128] + found[128:]
    at = (me % (128 // STRIDE)) * STRIDE + slot % STRIDE
    picked = jnp.sum(jnp.where(iota((128, hits), 0) == at, found, 0.0), axis=0, keepdims=True)
    logits = picked[:, : hits // 2] + picked[:, hits // 2 :]
    return jnp.concatenate([logits[:, n : n + 128] for n in range(0, hits // 2, 128)], axis=0)


def prep_kernel(step_no, steps, me_ref, slot_ref, got_ref, *refs):
    if step_no:
        old_table_ref, *refs = refs
        *refs, logits_ref = refs
        logits_ref[...] = own_logits(me_ref[0], old_table_ref, slot_ref[step_no - 1])
    turned_ref, cols_ref, *next_counts_ref = refs
    act_rows = turned_ref.shape[0]
    cols = columns(got_ref, step_no)
    cols_ref[...] = cols.astype(jnp.bfloat16)
    turned_ref[...] = lookups(cols, act_rows).T.astype(jnp.bfloat16)
    if next_counts_ref:
        next_cols = columns(got_ref, step_no + 1)
        next_counts_ref[0][...] = lookups(next_cols, act_rows).astype(jnp.bfloat16)


def prep(me, slot_of, got, old_table, step_no, act_rows):
    shards, steps, _, width = got.shape
    slots = shards * STRIDE
    outs = [
        jax.ShapeDtypeStruct((act_rows, slots), jnp.bfloat16),
        jax.ShapeDtypeStruct((slots, width), jnp.bfloat16),
    ]
    if step_no + 1 < steps:
        outs.append(jax.ShapeDtypeStruct((slots, act_rows), jnp.bfloat16))
    if step_no:
        outs.append(jax.ShapeDtypeStruct((slot_of.shape[2] // 256, 128), jnp.float32))
    args = [me, slot_of, got] + ([old_table] if step_no else [])
    return call(functools.partial(prep_kernel, step_no, steps), args, outs)


def weight_column(carried_ref, step_no, act_rows):
    row = carried_ref[act_rows + step_no : act_rows + step_no + 1, :]
    shape = (act_rows, row.shape[1])
    here = iota(shape, 1) == iota(shape, 0) // BLK
    return jnp.sum(jnp.where(here, row, 0.0), axis=1, keepdims=True)


def forward(weighted, counts, feats, mine_ref):
    width = feats.shape[1]
    products = halves(dot(counts, weighted)) * feats.astype(jnp.float32)
    same = iota((128, 128), 0) == iota((128, 128), 1)
    mine = []
    for k in range(mine_ref.shape[1]):
        column = jnp.sum(products[k * 128 : (k + 1) * 128], axis=1, keepdims=True) * width**-0.5
        mine.append(jnp.sum(jnp.where(same, column, 0.0), axis=0, keepdims=True))
    mine = jnp.concatenate(mine, axis=0)
    mine_ref[...] = jnp.broadcast_to(mine[None], mine_ref.shape)


def weigh_kernel(carried_ref, weighted_ref):
    act_rows = weighted_ref.shape[0]
    weighted_ref[...] = wide(weight_column(carried_ref, 0, act_rows) * carried_ref[:act_rows, :])


def first_kernel(weighted_ref, got_ref, mine_ref):
    counts = lookups(columns(got_ref, 0), weighted_ref.shape[0]).astype(jnp.bfloat16)
    forward(weighted_ref[...], counts, got_ref[:, 0].reshape(-1, got_ref.shape[3]), mine_ref)


def gradient(step_no, table_ref, mine_ref, cols_ref, got_ref, turned_ref, grad_ref):
    shards, blocks, _ = table_ref.shape
    width = got_ref.shape[3]
    feats = got_ref[:, step_no].reshape(-1, width)
    row, lane = iota((128, 128), 0), iota((128, 128), 1)
    base = (row // STRIDE) * STRIDE
    shard = iota((128, shards), 1).astype(jnp.float32)
    for k in range(blocks):
        cols = cols_ref[k * 128 : (k + 1) * 128, :].astype(jnp.float32)
        wanted = (shard == cols[:, 4:5]).astype(jnp.float32).astype(jnp.bfloat16)
        found = halves(dot(wanted, wide(table_ref[:, k, :])))
        partner = jnp.where(lane == base + cols[:, 5:6].astype(jnp.int32), found, 0.0)
        own = jnp.where(lane == row, mine_ref[0, k : k + 1, :], 0.0)
        error = jax.nn.sigmoid(jnp.sum(partner + own, axis=1, keepdims=True)) - cols[:, 6:7]
        part = error * feats[k * 128 : (k + 1) * 128].astype(jnp.float32) * width**-0.5
        grad_ref[k * 128 : (k + 1) * 128, :] = part.astype(jnp.bfloat16)
    return dot(turned_ref[...], grad_ref[...])


def step_kernel(
    step_no, carried_ref, rows_ref, table_ref, mine_ref, cols_ref, got_ref, turned_ref, next_counts_ref,
    new_rows_ref, new_mine_ref, grad_ref,
):
    act_rows, width = new_rows_ref.shape
    row_grad = gradient(step_no, table_ref, mine_ref, cols_ref, got_ref, turned_ref, grad_ref)
    rows = rows_ref[:act_rows, :] - step_rate * (weight_column(carried_ref, step_no, act_rows) * row_grad)
    new_rows_ref[...] = rows
    weighted = weight_column(carried_ref, step_no + 1, act_rows) * rows
    forward(wide(weighted), next_counts_ref[...], got_ref[:, step_no + 1].reshape(-1, width), new_mine_ref)


def last_kernel(
    step_no, me_ref, slot_ref, carried_ref, rows_ref, table_ref, mine_ref, cols_ref, got_ref, turned_ref,
    *refs,
):
    *known_refs, back_ref, grad_ref = refs
    act_rows = rows_ref.shape[0]
    row_grad = gradient(step_no, table_ref, mine_ref, cols_ref, got_ref, turned_ref, grad_ref)
    rows = rows_ref[...] - step_rate * (weight_column(carried_ref, step_no, act_rows) * row_grad)
    back_ref[:act_rows, :] = (rows - carried_ref[:act_rows, :]).astype(jnp.bfloat16)
    logits = own_logits(me_ref[0], table_ref, slot_ref[step_no])
    logits = jnp.concatenate([ref[...] for ref in known_refs] + [logits], axis=0)
    terms = [term.astype(jnp.float32) for term in split3(logits)]
    back_ref[act_rows:, :] = jnp.concatenate(terms + [jnp.zeros_like(logits)], axis=0).astype(jnp.bfloat16)


def call(kernel, args, outs, scratch=(), cost=None):
    smem, vmem = (pl.BlockSpec(memory_space=space) for space in (pltpu.SMEM, pltpu.VMEM))
    return pl.pallas_call(
        kernel,
        in_specs=[smem if arg.size == 1 else vmem for arg in args],
        out_specs=[vmem] * len(outs),
        out_shape=list(outs),
        scratch_shapes=list(scratch),
        compiler_params=pltpu.CompilerParams(vmem_limit_bytes=VMEM_LIMIT),
        cost_estimate=cost,
    )(*args)


def merge_kernel(blocks_ref, here_ref, table_ref, near_ref, far_ref, other_near_ref, other_far_ref, out_ref, sem):
    places, act_rows, _ = near_ref.shape
    places = 2 * places
    active = act_rows // BLK
    groups = 2 * places
    low = here_ref[0] == 0
    copy = pltpu.make_async_copy(table_ref, out_ref, sem)
    copy.start()
    copy.wait()

    def one(place, carry):
        apart = place ^ here_ref[1]
        part = ((apart >> 2) & 1) | (apart & 2)
        near = (apart & 1) == 0
        for c in range(2):
            own = low if c == 0 else jnp.logical_not(low)
            spots, values = [], []
            for slot in range(active):
                at = pl.ds(slot * BLK, BLK)
                mine = jnp.where(near, near_ref[part, at, :], far_ref[part, at, :])
                other = jnp.where(near, other_near_ref[part, at, :], other_far_ref[part, at, :])
                value = jnp.where(own, mine, other).astype(jnp.float32)
                spot = pl.ds(pl.multiple_of(blocks_ref[2 * place + c, slot] * BLK, BLK), BLK)
                spots.append(spot)
                values.append(out_ref[spot, :] + value * (1.0 / groups))
            for spot, value in zip(spots, values):
                out_ref[spot, :] = value
        return carry

    lax.fori_loop(0, places, one, 0)


def merge(blocks, here, table, held):
    smem, hbm = (pl.BlockSpec(memory_space=space) for space in (pltpu.SMEM, pltpu.HBM))
    whole = pl.BlockSpec(held[0].shape, lambda i: (0, 0, 0))
    return pl.pallas_call(
        merge_kernel,
        grid=(1,),
        in_specs=[smem, smem, hbm] + [whole] * 4,
        out_specs=pl.BlockSpec(table.shape, lambda i: (0, 0)),
        out_shape=jax.ShapeDtypeStruct(table.shape, jnp.float32),
        scratch_shapes=[pltpu.SemaphoreType.DMA],
        compiler_params=pltpu.CompilerParams(vmem_limit_bytes=MERGE_LIMIT),
    )(blocks, here, table, *held)


def body(turn, sizes, emb_table, active_blocks, hit_shards, lookup_slot, lookup_offset, block_weight, dense_feat, labels):
    shards = sizes["x"] * sizes["h"] * sizes["y"]
    _, steps, samples, _ = hit_shards.shape
    width = emb_table.shape[1]
    active = active_blocks.shape[2]
    act_rows = active * BLK
    slots = shards * STRIDE
    within = jnp.arange(BLK, dtype=jnp.int32)

    there = functools.partial(lax.ppermute, axis_name=HOME, perm=turn)
    looked = (lookup_slot[0] * BLK + lookup_offset[0] + 1).transpose(0, 2, 3, 1).reshape(steps, 8, samples)
    meta = jnp.concatenate(
        [
            hit_shards[0].transpose(0, 2, 1),
            looked,
            labels[0][:, None, :],
            jnp.zeros((steps, 5, samples), jnp.int32),
        ],
        axis=1,
    ).astype(jnp.bfloat16)
    meta = there(meta)
    feats = there(dense_feat[0])
    meta, blocks = lax.optimization_barrier((meta, active_blocks))
    my_blocks = blocks[lax.axis_index(("a1", "a0", "b", "c")), 0]
    local_index = (my_blocks[:, None] * BLK + within[None, :]).reshape(-1)
    weights = jnp.pad(block_weight[0, :, 0], ((0, 8 - steps), (0, width - active)))
    carried = there(jnp.concatenate([emb_table[local_index], weights], axis=0))

    packed, slot_of = pack(meta, feats, shards)
    got = lax.all_to_all(packed, GROUP, 0, 0, tiled=True)

    logit_rows = steps * samples // 128
    rows_like = jax.ShapeDtypeStruct((act_rows, width), jnp.float32)
    mine_like = jax.ShapeDtypeStruct((shards, slots // 128, 128), jnp.float32)
    back_like = jax.ShapeDtypeStruct((act_rows + 4 * logit_rows, width), jnp.bfloat16)
    scratch = [pltpu.VMEM((slots, width), jnp.bfloat16)]
    me = lax.axis_index(GROUP)[None]
    rows = carried
    weighted_like = jax.ShapeDtypeStruct((act_rows, 2 * width), jnp.bfloat16)
    (weighted,) = call(weigh_kernel, [carried], [weighted_like], cost=COVER)
    (mine,) = call(first_kernel, [weighted, got], [mine_like])
    table, known = None, []
    for t in range(steps):
        turned, cols, *more = prep(me, slot_of, got, table, t, act_rows)
        known += more[1:] if t + 1 < steps else more
        table = lax.all_to_all(mine, GROUP, 0, 0, tiled=True)
        if t + 1 < steps:
            rows, mine = call(
                functools.partial(step_kernel, t),
                [carried, rows, table, mine, cols, got, turned, more[0]],
                [rows_like, mine_like],
                scratch,
            )
        else:
            (back,) = call(
                functools.partial(last_kernel, t),
                [me, slot_of, carried, rows, table, mine, cols, got, turned, *known],
                [back_like],
                scratch,
            )

    back = there(back)
    delta, terms = back[:act_rows], back[act_rows:].astype(jnp.float32).reshape(4, logit_rows, 128)
    swap = [(0, 1), (1, 0)]
    for axis in ("a1", "a0"):
        delta = jnp.concatenate([delta, lax.ppermute(delta, axis, swap)], axis=0)
    held = [delta, lax.ppermute(delta, "b", swap)]
    held = [part.reshape(-1, act_rows, width) for part in held + [lax.ppermute(part, "c", swap) for part in held]]
    here = jnp.stack([lax.axis_index("c"), lax.axis_index(("a1", "a0", "b"))])
    new_table = merge(active_blocks[:, 0], here, emb_table, held)
    logits = (terms[0] + terms[1] + terms[2]).reshape(steps, samples)
    return new_table, logits[None]


def solution(mesh):
    shards = mesh.shape["shard"]
    y = min(4, shards // 4)
    sizes = {"a1": 2, "a0": 2, "b": 2, "c": 2, "x": shards // 4 // y, "h": 4, "y": y}
    finer = Mesh(mesh.devices.reshape(tuple(sizes.values())), tuple(sizes))
    index = lambda a, b, c, h: ((a * 2 + b) * 2 + c) * 4 + h
    turn = [
        (index(a, b, c, h), index(a ^ 2, h // 2, h % 2, b * 2 + c))
        for a in range(4)
        for b in range(2)
        for c in range(2)
        for h in range(4)
    ]
    group, shard = ("a1", "a0", "b", "c"), ("x", "h", "y")
    placed = (
        P(shard, None),
        P(None, shard, None),
        P(group, None, shard, None),
        P(group, None, shard, None, None),
        P(group, None, shard, None, None),
        P(group, None, shard, None),
        P(group, None, shard, None),
        P(group, None, shard),
    )
    return jax.shard_map(
        functools.partial(body, turn, sizes),
        mesh=finer,
        in_specs=placed,
        out_specs=(P(shard, None), P(group, None, shard)),
        check_vma=False,
    )
```

```python
import functools

import jax
import jax.numpy as jnp
from jax import lax
from jax.experimental import pallas as pl
from jax.experimental.pallas import tpu as pltpu
from jax.sharding import Mesh
from jax.sharding import PartitionSpec as P

BLK = 16
STRIDE = 16
META = 12
VMEM_LIMIT = 16 << 20
MERGE_LIMIT = 60 << 20

step_rate = 1.0

GROUP = ("x", "b", "c", "y")
HOME = ("a1", "a0", "b", "c", "h")


def split3(v):
    hi = v.astype(jnp.bfloat16)
    rest = v - hi.astype(jnp.float32)
    mid = rest.astype(jnp.bfloat16)
    return hi, mid, (rest - mid.astype(jnp.float32)).astype(jnp.bfloat16)


def wide(v):
    hi = v.astype(jnp.bfloat16)
    return jnp.concatenate([hi, (v - hi.astype(jnp.float32)).astype(jnp.bfloat16)], axis=1)


def halves(v):
    return v[:, : v.shape[1] // 2] + v[:, v.shape[1] // 2 :]


def dot(lhs, rhs, contract=((1,), (0,))):
    return lax.dot_general(lhs, rhs, (contract, ((), ())), preferred_element_type=jnp.float32)


def iota(shape, axis):
    return lax.broadcasted_iota(jnp.int32, shape, axis)


def pack_kernel(meta_ref, feat_ref, out_ref, slot_ref):
    shards, steps, _, width = out_ref.shape
    samples = feat_ref.shape[1]
    hits = 2 * samples
    before = (iota((hits, hits), 0) < iota((hits, hits), 1)).astype(jnp.float32).astype(jnp.bfloat16)
    at = iota((shards * STRIDE, samples), 0)
    at_row = iota((shards * STRIDE, shards), 0) == iota((shards * STRIDE, shards), 1) * STRIDE + META
    at_row = at_row.astype(jnp.float32).astype(jnp.bfloat16)
    for step_no in range(steps):
        parts = samples // width
        lines = meta_ref[step_no * parts * 16 : (step_no + 1) * parts * 16, :].astype(jnp.float32)
        meta = jnp.concatenate([lines[n * 16 : (n + 1) * 16] for n in range(parts)], axis=1)

        def pair(first, second):
            return jnp.concatenate([meta[first : first + 1], meta[second : second + 1]], axis=1)

        target = pair(0, 1).astype(jnp.int32)
        chosen = iota((shards, hits), 0) == target
        onehot = chosen.astype(jnp.float32).astype(jnp.bfloat16)
        rank = jnp.sum(jnp.where(chosen, dot(onehot, before), 0.0), axis=0, keepdims=True)
        rank_i = rank.astype(jnp.int32)
        slot = target * STRIDE + rank_i
        place = jnp.where((at == slot[:, :samples]) | (at == slot[:, samples:]), 1.0, 0.0).astype(jnp.bfloat16)
        packed = dot(place, feat_ref[step_no])
        other = jnp.concatenate([rank[:, samples:], rank[:, :samples]], axis=1)
        values = [pair(2 + n, 6 + n) for n in range(4)] + [pair(1, 0), other, pair(10, 10), jnp.ones_like(rank)]
        lane_of = iota((STRIDE, hits), 0) == rank_i
        spread = jnp.concatenate([jnp.where(lane_of, value, 0.0) for value in values], axis=0)
        rows = dot(onehot, spread.astype(jnp.bfloat16), ((1,), (1,)))
        packed = packed + dot(at_row, rows.astype(jnp.bfloat16))
        out_ref[:, step_no] = packed.astype(jnp.bfloat16).reshape(shards, STRIDE, width)
        slot_ref[step_no] = slot


def pack(meta, feats, shards):
    steps, samples, width = feats.shape
    return call(
        pack_kernel,
        [meta, feats],
        [
            jax.ShapeDtypeStruct((shards, steps, STRIDE, width), jnp.bfloat16),
            jax.ShapeDtypeStruct((steps, 1, 2 * samples), jnp.int32),
        ],
    )


def columns(got_ref, step_no):
    tiles = got_ref[:, step_no].astype(jnp.float32)
    width = tiles.shape[2]
    meta = jnp.broadcast_to(tiles[:, META : META + 1, :], tiles.shape).reshape(-1, width)
    own = iota(meta.shape, 1) % STRIDE == iota(meta.shape, 0) % STRIDE
    fold = iota((width, width), 0) // STRIDE == iota((width, width), 1)
    return dot(
        jnp.where(own, meta, 0.0).astype(jnp.bfloat16),
        fold.astype(jnp.float32).astype(jnp.bfloat16),
    )


def lookups(cols, act_rows):
    row_no = (iota((cols.shape[0], act_rows), 1) + 1).astype(jnp.float32)
    return sum(jnp.where(row_no == cols[:, n : n + 1], 1.0, 0.0) for n in range(4))


def own_logits(me, table_ref, slot):
    shards, blocks, _ = table_ref.shape
    hits = slot.shape[1]
    part = sum(jnp.where(me // (128 // STRIDE) == k, table_ref[:, k, :], 0.0) for k in range(blocks))
    onehot = iota((shards, hits), 0) == slot // STRIDE
    onehot = onehot.astype(jnp.float32).astype(jnp.bfloat16)
    found = dot(wide(part), onehot, ((0,), (0,)))
    found = found[:128] + found[128:]
    at = (me % (128 // STRIDE)) * STRIDE + slot % STRIDE
    picked = jnp.sum(jnp.where(iota((128, hits), 0) == at, found, 0.0), axis=0, keepdims=True)
    logits = picked[:, : hits // 2] + picked[:, hits // 2 :]
    return jnp.concatenate([logits[:, n : n + 128] for n in range(0, hits // 2, 128)], axis=0)


def prep_kernel(step_no, steps, me_ref, slot_ref, got_ref, *refs):
    if step_no:
        old_table_ref, *refs = refs
        *refs, logits_ref = refs
        logits_ref[...] = own_logits(me_ref[0], old_table_ref, slot_ref[step_no - 1])
    turned_ref, cols_ref, *next_counts_ref = refs
    act_rows = turned_ref.shape[0]
    cols = columns(got_ref, step_no)
    cols_ref[...] = cols.astype(jnp.bfloat16)
    turned_ref[...] = lookups(cols, act_rows).T.astype(jnp.bfloat16)
    if next_counts_ref:
        next_cols = columns(got_ref, step_no + 1)
        next_counts_ref[0][...] = lookups(next_cols, act_rows).astype(jnp.bfloat16)


def prep(me, slot_of, got, old_table, step_no, act_rows):
    shards, steps, _, width = got.shape
    slots = shards * STRIDE
    outs = [
        jax.ShapeDtypeStruct((act_rows, slots), jnp.bfloat16),
        jax.ShapeDtypeStruct((slots, width), jnp.bfloat16),
    ]
    if step_no + 1 < steps:
        outs.append(jax.ShapeDtypeStruct((slots, act_rows), jnp.bfloat16))
    if step_no:
        outs.append(jax.ShapeDtypeStruct((slot_of.shape[2] // 256, 128), jnp.float32))
    args = [me, slot_of, got] + ([old_table] if step_no else [])
    return call(functools.partial(prep_kernel, step_no, steps), args, outs)


def weight_column(carried_ref, step_no, act_rows):
    row = carried_ref[act_rows + step_no : act_rows + step_no + 1, :]
    shape = (act_rows, row.shape[1])
    here = iota(shape, 1) == iota(shape, 0) // BLK
    return jnp.sum(jnp.where(here, row, 0.0), axis=1, keepdims=True)


def forward(weighted, counts, feats, mine_ref, sent_ref):
    width = feats.shape[1]
    products = halves(dot(counts, weighted)) * feats.astype(jnp.float32)
    same = iota((128, 128), 0) == iota((128, 128), 1)
    mine = []
    for k in range(mine_ref.shape[0]):
        column = jnp.sum(products[k * 128 : (k + 1) * 128], axis=1, keepdims=True) * width**-0.5
        mine.append(jnp.sum(jnp.where(same, column, 0.0), axis=0, keepdims=True))
    mine = jnp.concatenate(mine, axis=0)
    mine_ref[...] = mine
    sent_ref[...] = jnp.broadcast_to(mine[None], sent_ref.shape)


def weigh_kernel(carried_ref, weighted_ref):
    act_rows = weighted_ref.shape[0]
    weighted_ref[...] = wide(weight_column(carried_ref, 0, act_rows) * carried_ref[:act_rows, :])


def first_kernel(weighted_ref, got_ref, mine_ref, sent_ref):
    counts = lookups(columns(got_ref, 0), weighted_ref.shape[0]).astype(jnp.bfloat16)
    forward(weighted_ref[...], counts, got_ref[:, 0].reshape(-1, got_ref.shape[3]), mine_ref, sent_ref)


def gradient(step_no, table_ref, mine_ref, cols_ref, got_ref, turned_ref, grad_ref):
    shards, blocks, _ = table_ref.shape
    width = got_ref.shape[3]
    feats = got_ref[:, step_no].reshape(-1, width)
    row, lane = iota((128, 128), 0), iota((128, 128), 1)
    base = (row // STRIDE) * STRIDE
    shard = iota((128, shards), 1).astype(jnp.float32)
    for k in range(blocks):
        cols = cols_ref[k * 128 : (k + 1) * 128, :].astype(jnp.float32)
        wanted = (shard == cols[:, 4:5]).astype(jnp.float32).astype(jnp.bfloat16)
        found = halves(dot(wanted, wide(table_ref[:, k, :])))
        partner = jnp.where(lane == base + cols[:, 5:6].astype(jnp.int32), found, 0.0)
        own = jnp.where(lane == row, mine_ref[k : k + 1, :], 0.0)
        error = jax.nn.sigmoid(jnp.sum(partner + own, axis=1, keepdims=True)) - cols[:, 6:7]
        part = error * feats[k * 128 : (k + 1) * 128].astype(jnp.float32) * width**-0.5
        grad_ref[k * 128 : (k + 1) * 128, :] = part.astype(jnp.bfloat16)
    return dot(turned_ref[...], grad_ref[...])


def step_kernel(
    step_no, carried_ref, rows_ref, table_ref, mine_ref, cols_ref, got_ref, turned_ref, next_counts_ref,
    new_rows_ref, new_mine_ref, sent_ref, grad_ref,
):
    act_rows, width = new_rows_ref.shape
    row_grad = gradient(step_no, table_ref, mine_ref, cols_ref, got_ref, turned_ref, grad_ref)
    rows = rows_ref[:act_rows, :] - step_rate * (weight_column(carried_ref, step_no, act_rows) * row_grad)
    new_rows_ref[...] = rows
    weighted = weight_column(carried_ref, step_no + 1, act_rows) * rows
    forward(wide(weighted), next_counts_ref[...], got_ref[:, step_no + 1].reshape(-1, width), new_mine_ref, sent_ref)


def last_kernel(
    step_no, me_ref, slot_ref, carried_ref, rows_ref, table_ref, mine_ref, cols_ref, got_ref, turned_ref,
    *refs,
):
    *known_refs, back_ref, grad_ref = refs
    act_rows = rows_ref.shape[0]
    row_grad = gradient(step_no, table_ref, mine_ref, cols_ref, got_ref, turned_ref, grad_ref)
    rows = rows_ref[...] - step_rate * (weight_column(carried_ref, step_no, act_rows) * row_grad)
    back_ref[:act_rows, :] = (rows - carried_ref[:act_rows, :]).astype(jnp.bfloat16)
    logits = own_logits(me_ref[0], table_ref, slot_ref[step_no])
    logits = jnp.concatenate([ref[...] for ref in known_refs] + [logits], axis=0)
    terms = [term.astype(jnp.float32) for term in split3(logits)]
    back_ref[act_rows:, :] = jnp.concatenate(terms + [jnp.zeros_like(logits)], axis=0).astype(jnp.bfloat16)


def call(kernel, args, outs, scratch=()):
    smem, vmem = (pl.BlockSpec(memory_space=space) for space in (pltpu.SMEM, pltpu.VMEM))
    return pl.pallas_call(
        kernel,
        in_specs=[smem if arg.size == 1 else vmem for arg in args],
        out_specs=[vmem] * len(outs),
        out_shape=list(outs),
        scratch_shapes=list(scratch),
        compiler_params=pltpu.CompilerParams(vmem_limit_bytes=VMEM_LIMIT),
    )(*args)


def merge_kernel(blocks_ref, here_ref, table_ref, near_ref, far_ref, other_near_ref, other_far_ref, out_ref, sem):
    places, act_rows, _ = near_ref.shape
    places = 2 * places
    active = act_rows // BLK
    groups = 2 * places
    low = here_ref[0] == 0
    copy = pltpu.make_async_copy(table_ref, out_ref, sem)
    copy.start()
    copy.wait()

    def one(place, carry):
        apart = place ^ here_ref[1]
        part = ((apart >> 2) & 1) | (apart & 2)
        near = (apart & 1) == 0
        for c in range(2):
            own = low if c == 0 else jnp.logical_not(low)
            spots, values = [], []
            for slot in range(active):
                at = pl.ds(slot * BLK, BLK)
                mine = jnp.where(near, near_ref[part, at, :], far_ref[part, at, :])
                other = jnp.where(near, other_near_ref[part, at, :], other_far_ref[part, at, :])
                value = jnp.where(own, mine, other).astype(jnp.float32)
                spot = pl.ds(pl.multiple_of(blocks_ref[2 * place + c, slot] * BLK, BLK), BLK)
                spots.append(spot)
                values.append(out_ref[spot, :] + value * (1.0 / groups))
            for spot, value in zip(spots, values):
                out_ref[spot, :] = value
        return carry

    lax.fori_loop(0, places, one, 0)


def merge(blocks, here, table, held):
    smem, hbm = (pl.BlockSpec(memory_space=space) for space in (pltpu.SMEM, pltpu.HBM))
    whole = pl.BlockSpec(held[0].shape, lambda i: (0, 0, 0))
    return pl.pallas_call(
        merge_kernel,
        grid=(1,),
        in_specs=[smem, smem, hbm] + [whole] * 4,
        out_specs=pl.BlockSpec(table.shape, lambda i: (0, 0)),
        out_shape=jax.ShapeDtypeStruct(table.shape, jnp.float32),
        scratch_shapes=[pltpu.SemaphoreType.DMA],
        compiler_params=pltpu.CompilerParams(vmem_limit_bytes=MERGE_LIMIT),
    )(blocks, here, table, *held)


def body(turn, sizes, emb_table, active_blocks, hit_shards, lookup_slot, lookup_offset, block_weight, dense_feat, labels):
    shards = sizes["x"] * sizes["h"] * sizes["y"]
    _, steps, samples, _ = hit_shards.shape
    width = emb_table.shape[1]
    active = active_blocks.shape[2]
    act_rows = active * BLK
    slots = shards * STRIDE
    within = jnp.arange(BLK, dtype=jnp.int32)

    there = functools.partial(lax.ppermute, axis_name=HOME, perm=turn)
    feats = there(dense_feat[0])
    looked = (lookup_slot[0] * BLK + lookup_offset[0] + 1).transpose(0, 2, 3, 1).reshape(steps, 8, samples)
    meta = [
        hit_shards[0].transpose(0, 2, 1),
        looked,
        labels[0][:, None, :],
        jnp.zeros((steps, 5, samples), jnp.int32),
    ]
    meta = jnp.concatenate(meta, axis=1).reshape(steps, 16, samples // width, width).transpose(0, 2, 1, 3)
    meta = meta.reshape(-1, width).astype(jnp.bfloat16)
    my_blocks = active_blocks[lax.axis_index(("a1", "a0", "b", "c")), 0]
    local_index = (my_blocks[:, None] * BLK + within[None, :]).reshape(-1)
    weights = jnp.pad(block_weight[0, :, 0], ((0, 8 - steps), (0, width - active)))
    rows = jnp.concatenate([emb_table[local_index], weights], axis=0)
    high = lax.reduce_precision(rows, 8, 7)
    rest = there(jnp.concatenate([meta, high.astype(jnp.bfloat16), (rows - high).astype(jnp.bfloat16)], axis=0))
    feats, rest = lax.optimization_barrier((feats, rest))
    meta, high, low = jnp.split(rest, [meta.shape[0], meta.shape[0] + rows.shape[0]])
    carried = high.astype(jnp.float32) + low.astype(jnp.float32)

    packed, slot_of = pack(meta, feats, shards)
    got = lax.all_to_all(packed, GROUP, 0, 0, tiled=True)

    logit_rows = steps * samples // 128
    rows_like = jax.ShapeDtypeStruct((act_rows, width), jnp.float32)
    mine_like = jax.ShapeDtypeStruct((slots // 128, 128), jnp.float32)
    sent_like = jax.ShapeDtypeStruct((shards, slots // 128, 128), jnp.float32)
    back_like = jax.ShapeDtypeStruct((act_rows + 4 * logit_rows, width), jnp.bfloat16)
    scratch = [pltpu.VMEM((slots, width), jnp.bfloat16)]
    me = lax.axis_index(GROUP)[None]
    rows = carried
    weighted_like = jax.ShapeDtypeStruct((act_rows, 2 * width), jnp.bfloat16)
    (weighted,) = call(weigh_kernel, [carried], [weighted_like])
    mine, sent = call(first_kernel, [weighted, got], [mine_like, sent_like])
    table, known = None, []
    for t in range(steps):
        turned, cols, *more = prep(me, slot_of, got, table, t, act_rows)
        known += more[1:] if t + 1 < steps else more
        table = lax.all_to_all(sent, GROUP, 0, 0, tiled=True)
        if t + 1 < steps:
            rows, mine, sent = call(
                functools.partial(step_kernel, t),
                [carried, rows, table, mine, cols, got, turned, more[0]],
                [rows_like, mine_like, sent_like],
                scratch,
            )
        else:
            (back,) = call(
                functools.partial(last_kernel, t),
                [me, slot_of, carried, rows, table, mine, cols, got, turned, *known],
                [back_like],
                scratch,
            )

    back = there(back)
    delta, terms = back[:act_rows], back[act_rows:].astype(jnp.float32).reshape(4, logit_rows, 128)
    swap = [(0, 1), (1, 0)]
    for axis in ("a1", "a0"):
        delta = jnp.concatenate([delta, lax.ppermute(delta, axis, swap)], axis=0)
    held = [delta, lax.ppermute(delta, "b", swap)]
    held = [part.reshape(-1, act_rows, width) for part in held + [lax.ppermute(part, "c", swap) for part in held]]
    here = jnp.stack([lax.axis_index("c"), lax.axis_index(("a1", "a0", "b"))])
    new_table = merge(active_blocks[:, 0], here, emb_table, held)
    logits = (terms[0] + terms[1] + terms[2]).reshape(steps, samples)
    return new_table, logits[None]


def solution(mesh):
    shards = mesh.shape["shard"]
    y = min(4, shards // 4)
    sizes = {"a1": 2, "a0": 2, "b": 2, "c": 2, "x": shards // 4 // y, "h": 4, "y": y}
    finer = Mesh(mesh.devices.reshape(tuple(sizes.values())), tuple(sizes))
    index = lambda a, b, c, h: ((a * 2 + b) * 2 + c) * 4 + h
    turn = [
        (index(a, b, c, h), index(a ^ 2, h // 2, h % 2, b * 2 + c))
        for a in range(4)
        for b in range(2)
        for c in range(2)
        for h in range(4)
    ]
    group, shard = ("a1", "a0", "b", "c"), ("x", "h", "y")
    placed = (
        P(shard, None),
        P(None, shard, None),
        P(group, None, shard, None),
        P(group, None, shard, None, None),
        P(group, None, shard, None, None),
        P(group, None, shard, None),
        P(group, None, shard, None),
        P(group, None, shard),
    )
    return jax.shard_map(
        functools.partial(body, turn, sizes),
        mesh=finer,
        in_specs=placed,
        out_specs=(P(shard, None), P(group, None, shard)),
        check_vma=False,
    )
```

```python
import functools

import jax
import jax.numpy as jnp
from jax import lax
from jax.experimental import pallas as pl
from jax.experimental.pallas import tpu as pltpu
from jax.sharding import Mesh
from jax.sharding import PartitionSpec as P

BLK = 16
STRIDE = 16
META = 12
VMEM_LIMIT = 16 << 20
MERGE_LIMIT = 51 << 20

step_rate = 1.0

GROUP = ("x", "b", "c", "y")
HOME = ("a1", "a0", "b", "c", "h")


def split3(v):
    hi = v.astype(jnp.bfloat16)
    rest = v - hi.astype(jnp.float32)
    mid = rest.astype(jnp.bfloat16)
    return hi, mid, (rest - mid.astype(jnp.float32)).astype(jnp.bfloat16)


def wide(v):
    hi = v.astype(jnp.bfloat16)
    return jnp.concatenate([hi, (v - hi.astype(jnp.float32)).astype(jnp.bfloat16)], axis=1)


def halves(v):
    return v[:, : v.shape[1] // 2] + v[:, v.shape[1] // 2 :]


def dot(lhs, rhs, contract=((1,), (0,))):
    return lax.dot_general(lhs, rhs, (contract, ((), ())), preferred_element_type=jnp.float32)


def iota(shape, axis):
    return lax.broadcasted_iota(jnp.int32, shape, axis)


def pack_kernel(meta_ref, feat_ref, out_ref, slot_ref):
    shards, steps, _, width = out_ref.shape
    samples = feat_ref.shape[1]
    hits = 2 * samples
    before = (iota((hits, hits), 0) < iota((hits, hits), 1)).astype(jnp.float32).astype(jnp.bfloat16)
    at = iota((shards * STRIDE, samples), 0)
    at_row = iota((shards * STRIDE, shards), 0) == iota((shards * STRIDE, shards), 1) * STRIDE + META
    at_row = at_row.astype(jnp.float32).astype(jnp.bfloat16)
    meta = meta_ref[...].astype(jnp.float32)
    for step_no in range(steps):

        def pair(first, second):
            parts = samples // width
            lines = [(value * steps + step_no) * parts + n for value in (first, second) for n in range(parts)]
            return jnp.concatenate([meta[line : line + 1] for line in lines], axis=1)

        target = pair(0, 1).astype(jnp.int32)
        chosen = iota((shards, hits), 0) == target
        onehot = chosen.astype(jnp.float32).astype(jnp.bfloat16)
        rank = jnp.sum(jnp.where(chosen, dot(onehot, before), 0.0), axis=0, keepdims=True)
        rank_i = rank.astype(jnp.int32)
        slot = target * STRIDE + rank_i
        place = jnp.where((at == slot[:, :samples]) | (at == slot[:, samples:]), 1.0, 0.0).astype(jnp.bfloat16)
        packed = dot(place, feat_ref[step_no])
        other = jnp.concatenate([rank[:, samples:], rank[:, :samples]], axis=1)
        values = [pair(2 + n, 6 + n) for n in range(4)] + [pair(1, 0), other, pair(10, 10), jnp.ones_like(rank)]
        lane_of = iota((STRIDE, hits), 0) == rank_i
        spread = jnp.concatenate([jnp.where(lane_of, value, 0.0) for value in values], axis=0)
        rows = dot(onehot, spread.astype(jnp.bfloat16), ((1,), (1,)))
        packed = packed + dot(at_row, rows.astype(jnp.bfloat16))
        out_ref[:, step_no] = packed.astype(jnp.bfloat16).reshape(shards, STRIDE, width)
        slot_ref[step_no] = slot


def pack(meta, feats, shards):
    steps, samples, width = feats.shape
    return call(
        pack_kernel,
        [meta, feats],
        [
            jax.ShapeDtypeStruct((shards, steps, STRIDE, width), jnp.bfloat16),
            jax.ShapeDtypeStruct((steps, 1, 2 * samples), jnp.int32),
        ],
    )


def columns(got_ref, step_no):
    tiles = got_ref[:, step_no].astype(jnp.float32)
    width = tiles.shape[2]
    meta = jnp.broadcast_to(tiles[:, META : META + 1, :], tiles.shape).reshape(-1, width)
    own = iota(meta.shape, 1) % STRIDE == iota(meta.shape, 0) % STRIDE
    fold = iota((width, width), 0) // STRIDE == iota((width, width), 1)
    return dot(
        jnp.where(own, meta, 0.0).astype(jnp.bfloat16),
        fold.astype(jnp.float32).astype(jnp.bfloat16),
    )


def lookups(cols, act_rows):
    row_no = (iota((cols.shape[0], act_rows), 1) + 1).astype(jnp.float32)
    return sum(jnp.where(row_no == cols[:, n : n + 1], 1.0, 0.0) for n in range(4))


def own_logits(me, table_ref, slot):
    shards, blocks, _ = table_ref.shape
    hits = slot.shape[1]
    part = sum(jnp.where(me // (128 // STRIDE) == k, table_ref[:, k, :], 0.0) for k in range(blocks))
    onehot = iota((shards, hits), 0) == slot // STRIDE
    onehot = onehot.astype(jnp.float32).astype(jnp.bfloat16)
    found = dot(wide(part), onehot, ((0,), (0,)))
    found = found[:128] + found[128:]
    at = (me % (128 // STRIDE)) * STRIDE + slot % STRIDE
    picked = jnp.sum(jnp.where(iota((128, hits), 0) == at, found, 0.0), axis=0, keepdims=True)
    logits = picked[:, : hits // 2] + picked[:, hits // 2 :]
    return jnp.concatenate([logits[:, n : n + 128] for n in range(0, hits // 2, 128)], axis=0)


def prep_kernel(step_no, steps, me_ref, slot_ref, got_ref, *refs):
    if step_no:
        old_table_ref, *refs = refs
        *refs, logits_ref = refs
        logits_ref[...] = own_logits(me_ref[0], old_table_ref, slot_ref[step_no - 1])
    turned_ref, cols_ref, *next_counts_ref = refs
    act_rows = turned_ref.shape[0]
    cols = columns(got_ref, step_no)
    cols_ref[...] = cols.astype(jnp.bfloat16)
    turned_ref[...] = lookups(cols, act_rows).T.astype(jnp.bfloat16)
    if next_counts_ref:
        next_cols = columns(got_ref, step_no + 1)
        next_counts_ref[0][...] = lookups(next_cols, act_rows).astype(jnp.bfloat16)


def prep(me, slot_of, got, old_table, step_no, act_rows):
    shards, steps, _, width = got.shape
    slots = shards * STRIDE
    outs = [
        jax.ShapeDtypeStruct((act_rows, slots), jnp.bfloat16),
        jax.ShapeDtypeStruct((slots, width), jnp.bfloat16),
    ]
    if step_no + 1 < steps:
        outs.append(jax.ShapeDtypeStruct((slots, act_rows), jnp.bfloat16))
    if step_no:
        outs.append(jax.ShapeDtypeStruct((slot_of.shape[2] // 256, 128), jnp.float32))
    args = [me, slot_of, got] + ([old_table] if step_no else [])
    return call(functools.partial(prep_kernel, step_no, steps), args, outs)


def weight_column(carried_ref, step_no, act_rows):
    row = carried_ref[act_rows + step_no : act_rows + step_no + 1, :]
    shape = (act_rows, row.shape[1])
    here = iota(shape, 1) == iota(shape, 0) // BLK
    return jnp.sum(jnp.where(here, row, 0.0), axis=1, keepdims=True)


def forward(weighted, counts, feats, mine_ref, sent_ref):
    width = feats.shape[1]
    products = halves(dot(counts, weighted)) * feats.astype(jnp.float32)
    same = iota((128, 128), 0) == iota((128, 128), 1)
    mine = []
    for k in range(mine_ref.shape[0]):
        column = jnp.sum(products[k * 128 : (k + 1) * 128], axis=1, keepdims=True) * width**-0.5
        mine.append(jnp.sum(jnp.where(same, column, 0.0), axis=0, keepdims=True))
    mine = jnp.concatenate(mine, axis=0)
    mine_ref[...] = mine
    sent_ref[...] = jnp.broadcast_to(mine[None], sent_ref.shape)


def weigh_kernel(carried_ref, weighted_ref):
    act_rows = weighted_ref.shape[0]
    weighted_ref[...] = wide(weight_column(carried_ref, 0, act_rows) * carried_ref[:act_rows, :])


def first_kernel(weighted_ref, got_ref, mine_ref, sent_ref):
    counts = lookups(columns(got_ref, 0), weighted_ref.shape[0]).astype(jnp.bfloat16)
    forward(weighted_ref[...], counts, got_ref[:, 0].reshape(-1, got_ref.shape[3]), mine_ref, sent_ref)


def gradient(step_no, table_ref, mine_ref, cols_ref, got_ref, turned_ref, grad_ref):
    shards, blocks, _ = table_ref.shape
    width = got_ref.shape[3]
    feats = got_ref[:, step_no].reshape(-1, width)
    row, lane = iota((128, 128), 0), iota((128, 128), 1)
    base = (row // STRIDE) * STRIDE
    shard = iota((128, shards), 1).astype(jnp.float32)
    for k in range(blocks):
        cols = cols_ref[k * 128 : (k + 1) * 128, :].astype(jnp.float32)
        wanted = (shard == cols[:, 4:5]).astype(jnp.float32).astype(jnp.bfloat16)
        found = halves(dot(wanted, wide(table_ref[:, k, :])))
        partner = jnp.where(lane == base + cols[:, 5:6].astype(jnp.int32), found, 0.0)
        own = jnp.where(lane == row, mine_ref[k : k + 1, :], 0.0)
        error = jax.nn.sigmoid(jnp.sum(partner + own, axis=1, keepdims=True)) - cols[:, 6:7]
        part = error * feats[k * 128 : (k + 1) * 128].astype(jnp.float32) * width**-0.5
        grad_ref[k * 128 : (k + 1) * 128, :] = part.astype(jnp.bfloat16)
    return dot(turned_ref[...], grad_ref[...])


def step_kernel(
    step_no, carried_ref, rows_ref, table_ref, mine_ref, cols_ref, got_ref, turned_ref, next_counts_ref,
    new_rows_ref, new_mine_ref, sent_ref, grad_ref,
):
    act_rows, width = new_rows_ref.shape
    row_grad = gradient(step_no, table_ref, mine_ref, cols_ref, got_ref, turned_ref, grad_ref)
    rows = rows_ref[:act_rows, :] - step_rate * (weight_column(carried_ref, step_no, act_rows) * row_grad)
    new_rows_ref[...] = rows
    weighted = weight_column(carried_ref, step_no + 1, act_rows) * rows
    forward(wide(weighted), next_counts_ref[...], got_ref[:, step_no + 1].reshape(-1, width), new_mine_ref, sent_ref)


def last_kernel(
    step_no, me_ref, slot_ref, carried_ref, rows_ref, table_ref, mine_ref, cols_ref, got_ref, turned_ref,
    *refs,
):
    *known_refs, back_ref, grad_ref = refs
    act_rows = rows_ref.shape[0]
    row_grad = gradient(step_no, table_ref, mine_ref, cols_ref, got_ref, turned_ref, grad_ref)
    rows = rows_ref[...] - step_rate * (weight_column(carried_ref, step_no, act_rows) * row_grad)
    back_ref[:act_rows, :] = (rows - carried_ref[:act_rows, :]).astype(jnp.bfloat16)
    logits = own_logits(me_ref[0], table_ref, slot_ref[step_no])
    logits = jnp.concatenate([ref[...] for ref in known_refs] + [logits], axis=0)
    terms = [term.astype(jnp.float32) for term in split3(logits)]
    back_ref[act_rows:, :] = jnp.concatenate(terms + [jnp.zeros_like(logits)], axis=0).astype(jnp.bfloat16)


def call(kernel, args, outs, scratch=()):
    smem, vmem = (pl.BlockSpec(memory_space=space) for space in (pltpu.SMEM, pltpu.VMEM))
    return pl.pallas_call(
        kernel,
        in_specs=[smem if arg.size == 1 else vmem for arg in args],
        out_specs=[vmem] * len(outs),
        out_shape=list(outs),
        scratch_shapes=list(scratch),
        compiler_params=pltpu.CompilerParams(vmem_limit_bytes=VMEM_LIMIT),
    )(*args)


def merge_kernel(blocks_ref, here_ref, table_ref, near_ref, far_ref, other_near_ref, other_far_ref, out_ref, sem):
    places, act_rows, _ = near_ref.shape
    places = 2 * places
    active = act_rows // BLK
    groups = 2 * places
    low = here_ref[0] == 0
    copy = pltpu.make_async_copy(table_ref, out_ref, sem)
    copy.start()
    copy.wait()

    def one(place, carry):
        apart = place ^ here_ref[1]
        part = ((apart >> 2) & 1) | (apart & 2)
        near = (apart & 1) == 0
        for c in range(2):
            own = low if c == 0 else jnp.logical_not(low)
            spots, values = [], []
            for slot in range(active):
                at = pl.ds(slot * BLK, BLK)
                mine = jnp.where(near, near_ref[part, at, :], far_ref[part, at, :])
                other = jnp.where(near, other_near_ref[part, at, :], other_far_ref[part, at, :])
                value = jnp.where(own, mine, other).astype(jnp.float32)
                spot = pl.ds(pl.multiple_of(blocks_ref[2 * place + c, slot] * BLK, BLK), BLK)
                spots.append(spot)
                values.append(out_ref[spot, :] + value * (1.0 / groups))
            for spot, value in zip(spots, values):
                out_ref[spot, :] = value
        return carry

    lax.fori_loop(0, places, one, 0)


def merge(blocks, here, table, held):
    smem, hbm = (pl.BlockSpec(memory_space=space) for space in (pltpu.SMEM, pltpu.HBM))
    whole = pl.BlockSpec(memory_space=pltpu.VMEM)
    return pl.pallas_call(
        merge_kernel,
        grid=(1,),
        in_specs=[smem, smem, hbm] + [whole] * 4,
        out_specs=pl.BlockSpec(table.shape, lambda i: (0, 0)),
        out_shape=jax.ShapeDtypeStruct(table.shape, jnp.float32),
        scratch_shapes=[pltpu.SemaphoreType.DMA],
        compiler_params=pltpu.CompilerParams(vmem_limit_bytes=MERGE_LIMIT),
    )(blocks, here, table, *held)


def body(turn, sizes, emb_table, active_blocks, hit_shards, lookup_slot, lookup_offset, block_weight, dense_feat, labels):
    shards = sizes["x"] * sizes["h"] * sizes["y"]
    _, steps, samples, _ = hit_shards.shape
    width = emb_table.shape[1]
    active = active_blocks.shape[2]
    act_rows = active * BLK
    slots = shards * STRIDE
    within = jnp.arange(BLK, dtype=jnp.int32)

    there = functools.partial(lax.ppermute, axis_name=HOME, perm=turn)
    feats = there(dense_feat[0])
    looked = (lookup_slot[0] * BLK + lookup_offset[0] + 1).transpose(2, 3, 0, 1).reshape(-1, steps, samples)
    meta = jnp.concatenate([hit_shards[0].transpose(2, 0, 1), looked, labels[0][None]], axis=0)
    meta = meta.reshape(-1, width).astype(jnp.bfloat16)
    my_blocks = active_blocks[lax.axis_index(("a1", "a0", "b", "c")), 0]
    local_index = (my_blocks[:, None] * BLK + within[None, :]).reshape(-1)
    weights = jnp.pad(block_weight[0, :, 0], ((0, 0), (0, width - active)))
    parts = [meta]
    for exact in (weights, emb_table[local_index]):
        high = lax.reduce_precision(exact, 8, 7)
        parts += [high.astype(jnp.bfloat16), (exact - high).astype(jnp.bfloat16)]
    rest = there(jnp.concatenate(parts, axis=0))
    feats, rest = lax.optimization_barrier((feats, rest))
    ends = [sum(part.shape[0] for part in parts[: n + 1]) for n in range(len(parts) - 1)]
    meta, *terms = [part.astype(jnp.float32) for part in jnp.split(rest, ends)]
    meta = meta.astype(jnp.bfloat16)
    weights = jnp.pad(terms[0] + terms[1], ((0, 8 - steps), (0, 0)))
    carried = jnp.concatenate([terms[2] + terms[3], weights], axis=0)

    packed, slot_of = pack(meta, feats, shards)
    got = lax.all_to_all(packed, GROUP, 0, 0, tiled=True)

    logit_rows = steps * samples // 128
    rows_like = jax.ShapeDtypeStruct((act_rows, width), jnp.float32)
    mine_like = jax.ShapeDtypeStruct((slots // 128, 128), jnp.float32)
    sent_like = jax.ShapeDtypeStruct((shards, slots // 128, 128), jnp.float32)
    back_like = jax.ShapeDtypeStruct((act_rows + 4 * logit_rows, width), jnp.bfloat16)
    scratch = [pltpu.VMEM((slots, width), jnp.bfloat16)]
    me = lax.axis_index(GROUP)[None]
    rows = carried
    weighted_like = jax.ShapeDtypeStruct((act_rows, 2 * width), jnp.bfloat16)
    (weighted,) = call(weigh_kernel, [carried], [weighted_like])
    mine, sent = call(first_kernel, [weighted, got], [mine_like, sent_like])
    table, known = None, []
    for t in range(steps):
        turned, cols, *more = prep(me, slot_of, got, table, t, act_rows)
        known += more[1:] if t + 1 < steps else more
        table = lax.all_to_all(sent, GROUP, 0, 0, tiled=True)
        if t + 1 < steps:
            rows, mine, sent = call(
                functools.partial(step_kernel, t),
                [carried, rows, table, mine, cols, got, turned, more[0]],
                [rows_like, mine_like, sent_like],
                scratch,
            )
        else:
            (back,) = call(
                functools.partial(last_kernel, t),
                [me, slot_of, carried, rows, table, mine, cols, got, turned, *known],
                [back_like],
                scratch,
            )

    back = there(back)
    delta, terms = back[:act_rows], back[act_rows:].astype(jnp.float32).reshape(4, logit_rows, 128)
    swap = [(0, 1), (1, 0)]
    for axis in ("a1", "a0"):
        delta = jnp.concatenate([delta, lax.ppermute(delta, axis, swap)], axis=0)
    held = [delta, lax.ppermute(delta, "b", swap)]
    held = [part.reshape(-1, act_rows, width) for part in held + [lax.ppermute(part, "c", swap) for part in held]]
    here = jnp.stack([lax.axis_index("c"), lax.axis_index(("a1", "a0", "b"))])
    new_table = merge(active_blocks[:, 0], here, emb_table, held)
    logits = (terms[0] + terms[1] + terms[2]).reshape(steps, samples)
    return new_table, logits[None]


def solution(mesh):
    shards = mesh.shape["shard"]
    y = min(4, shards // 4)
    sizes = {"a1": 2, "a0": 2, "b": 2, "c": 2, "x": shards // 4 // y, "h": 4, "y": y}
    finer = Mesh(mesh.devices.reshape(tuple(sizes.values())), tuple(sizes))
    index = lambda a, b, c, h: ((a * 2 + b) * 2 + c) * 4 + h
    turn = [
        (index(a, b, c, h), index(a ^ 2, h // 2, h % 2, b * 2 + c))
        for a in range(4)
        for b in range(2)
        for c in range(2)
        for h in range(4)
    ]
    group, shard = ("a1", "a0", "b", "c"), ("x", "h", "y")
    placed = (
        P(shard, None),
        P(None, shard, None),
        P(group, None, shard, None),
        P(group, None, shard, None, None),
        P(group, None, shard, None, None),
        P(group, None, shard, None),
        P(group, None, shard, None),
        P(group, None, shard),
    )
    return jax.shard_map(
        functools.partial(body, turn, sizes),
        mesh=finer,
        in_specs=placed,
        out_specs=(P(shard, None), P(group, None, shard)),
        check_vma=False,
    )
```

```python
import functools

import jax
import jax.numpy as jnp
from jax import lax
from jax.experimental import pallas as pl
from jax.experimental.pallas import tpu as pltpu
from jax.sharding import Mesh
from jax.sharding import PartitionSpec as P

BLK = 16
STRIDE = 16
META = 12
VMEM_LIMIT = 16 << 20
MERGE_LIMIT = 51 << 20

step_rate = 1.0

GROUP = ("x", "b", "c", "y")
HOME = ("a1", "a0", "b", "c", "h")


def split3(v):
    hi = v.astype(jnp.bfloat16)
    rest = v - hi.astype(jnp.float32)
    mid = rest.astype(jnp.bfloat16)
    return hi, mid, (rest - mid.astype(jnp.float32)).astype(jnp.bfloat16)


def wide(v):
    hi = v.astype(jnp.bfloat16)
    return jnp.concatenate([hi, (v - hi.astype(jnp.float32)).astype(jnp.bfloat16)], axis=1)


def halves(v):
    return v[:, : v.shape[1] // 2] + v[:, v.shape[1] // 2 :]


def dot(lhs, rhs, contract=((1,), (0,))):
    return lax.dot_general(lhs, rhs, (contract, ((), ())), preferred_element_type=jnp.float32)


def iota(shape, axis):
    return lax.broadcasted_iota(jnp.int32, shape, axis)


def pack_kernel(meta_ref, feat_ref, out_ref, slot_ref):
    shards, steps, _, width = out_ref.shape
    samples = feat_ref.shape[1]
    hits = 2 * samples
    before = (iota((hits, hits), 0) < iota((hits, hits), 1)).astype(jnp.float32).astype(jnp.bfloat16)
    at = iota((shards * STRIDE, samples), 0)
    at_row = iota((shards * STRIDE, shards), 0) == iota((shards * STRIDE, shards), 1) * STRIDE + META
    at_row = at_row.astype(jnp.float32).astype(jnp.bfloat16)
    meta = meta_ref[...].astype(jnp.float32)
    for step_no in range(steps):

        def pair(first, second):
            parts = samples // width
            lines = [(value * steps + step_no) * parts + n for value in (first, second) for n in range(parts)]
            return jnp.concatenate([meta[line : line + 1] for line in lines], axis=1)

        target = pair(0, 1).astype(jnp.int32)
        chosen = iota((shards, hits), 0) == target
        onehot = chosen.astype(jnp.float32).astype(jnp.bfloat16)
        rank = jnp.sum(jnp.where(chosen, dot(onehot, before), 0.0), axis=0, keepdims=True)
        rank_i = rank.astype(jnp.int32)
        slot = target * STRIDE + rank_i
        place = jnp.where((at == slot[:, :samples]) | (at == slot[:, samples:]), 1.0, 0.0).astype(jnp.bfloat16)
        packed = dot(place, feat_ref[step_no])
        other = jnp.concatenate([rank[:, samples:], rank[:, :samples]], axis=1)
        values = [pair(2 + n, 6 + n) for n in range(4)] + [pair(1, 0), other, pair(10, 10), jnp.ones_like(rank)]
        lane_of = iota((STRIDE, hits), 0) == rank_i
        spread = jnp.concatenate([jnp.where(lane_of, value, 0.0) for value in values], axis=0)
        rows = dot(onehot, spread.astype(jnp.bfloat16), ((1,), (1,)))
        packed = packed + dot(at_row, rows.astype(jnp.bfloat16))
        out_ref[:, step_no] = packed.astype(jnp.bfloat16).reshape(shards, STRIDE, width)
        slot_ref[step_no] = slot


def pack(meta, feats, shards):
    steps, samples, width = feats.shape
    return call(
        pack_kernel,
        [meta, feats],
        [
            jax.ShapeDtypeStruct((shards, steps, STRIDE, width), jnp.bfloat16),
            jax.ShapeDtypeStruct((steps, 1, 2 * samples), jnp.int32),
        ],
    )


def columns(got_ref, step_no):
    tiles = got_ref[:, step_no].astype(jnp.float32)
    width = tiles.shape[2]
    meta = jnp.broadcast_to(tiles[:, META : META + 1, :], tiles.shape).reshape(-1, width)
    own = iota(meta.shape, 1) % STRIDE == iota(meta.shape, 0) % STRIDE
    fold = iota((width, width), 0) // STRIDE == iota((width, width), 1)
    return dot(
        jnp.where(own, meta, 0.0).astype(jnp.bfloat16),
        fold.astype(jnp.float32).astype(jnp.bfloat16),
    )


def lookups(cols, act_rows):
    row_no = (iota((cols.shape[0], act_rows), 1) + 1).astype(jnp.float32)
    return sum(jnp.where(row_no == cols[:, n : n + 1], 1.0, 0.0) for n in range(4))


def own_logits(me, table_ref, slot):
    shards, blocks, _ = table_ref.shape
    hits = slot.shape[1]
    part = sum(jnp.where(me // (128 // STRIDE) == k, table_ref[:, k, :], 0.0) for k in range(blocks))
    onehot = iota((shards, hits), 0) == slot // STRIDE
    onehot = onehot.astype(jnp.float32).astype(jnp.bfloat16)
    found = dot(wide(part), onehot, ((0,), (0,)))
    found = found[:128] + found[128:]
    at = (me % (128 // STRIDE)) * STRIDE + slot % STRIDE
    picked = jnp.sum(jnp.where(iota((128, hits), 0) == at, found, 0.0), axis=0, keepdims=True)
    logits = picked[:, : hits // 2] + picked[:, hits // 2 :]
    return jnp.concatenate([logits[:, n : n + 128] for n in range(0, hits // 2, 128)], axis=0)


def prep_kernel(step_no, steps, me_ref, slot_ref, got_ref, *refs):
    if step_no:
        old_table_ref, *refs = refs
        *refs, logits_ref = refs
        logits_ref[...] = own_logits(me_ref[0], old_table_ref, slot_ref[step_no - 1])
    turned_ref, cols_ref, *next_counts_ref = refs
    act_rows = turned_ref.shape[0]
    cols = columns(got_ref, step_no)
    cols_ref[...] = cols.astype(jnp.bfloat16)
    turned_ref[...] = lookups(cols, act_rows).T.astype(jnp.bfloat16)
    if next_counts_ref:
        next_cols = columns(got_ref, step_no + 1)
        next_counts_ref[0][...] = lookups(next_cols, act_rows).astype(jnp.bfloat16)


def prep(me, slot_of, got, old_table, step_no, act_rows):
    shards, steps, _, width = got.shape
    slots = shards * STRIDE
    outs = [
        jax.ShapeDtypeStruct((act_rows, slots), jnp.bfloat16),
        jax.ShapeDtypeStruct((slots, width), jnp.bfloat16),
    ]
    if step_no + 1 < steps:
        outs.append(jax.ShapeDtypeStruct((slots, act_rows), jnp.bfloat16))
    if step_no:
        outs.append(jax.ShapeDtypeStruct((slot_of.shape[2] // 256, 128), jnp.float32))
    args = [me, slot_of, got] + ([old_table] if step_no else [])
    return call(functools.partial(prep_kernel, step_no, steps), args, outs)


def weight_column(carried_ref, step_no, act_rows):
    row = carried_ref[act_rows + step_no : act_rows + step_no + 1, :]
    shape = (act_rows, row.shape[1])
    here = iota(shape, 1) == iota(shape, 0) // BLK
    return jnp.sum(jnp.where(here, row, 0.0), axis=1, keepdims=True)


def forward(weighted, counts, feats, mine_ref, sent_ref):
    width = feats.shape[1]
    products = halves(dot(counts, weighted)) * feats.astype(jnp.float32)
    same = iota((128, 128), 0) == iota((128, 128), 1)
    mine = []
    for k in range(mine_ref.shape[0]):
        column = jnp.sum(products[k * 128 : (k + 1) * 128], axis=1, keepdims=True) * width**-0.5
        mine.append(jnp.sum(jnp.where(same, column, 0.0), axis=0, keepdims=True))
    mine = jnp.concatenate(mine, axis=0)
    mine_ref[...] = mine
    sent_ref[...] = jnp.broadcast_to(mine[None], sent_ref.shape)


def weigh_kernel(carried_ref, weighted_ref):
    act_rows = weighted_ref.shape[0]
    weighted_ref[...] = wide(weight_column(carried_ref, 0, act_rows) * carried_ref[:act_rows, :])


def first_kernel(weighted_ref, got_ref, mine_ref, sent_ref):
    counts = lookups(columns(got_ref, 0), weighted_ref.shape[0]).astype(jnp.bfloat16)
    forward(weighted_ref[...], counts, got_ref[:, 0].reshape(-1, got_ref.shape[3]), mine_ref, sent_ref)


def gradient(step_no, table_ref, mine_ref, cols_ref, got_ref, turned_ref, grad_ref):
    shards, blocks, _ = table_ref.shape
    width = got_ref.shape[3]
    feats = got_ref[:, step_no].reshape(-1, width)
    row, lane = iota((128, 128), 0), iota((128, 128), 1)
    base = (row // STRIDE) * STRIDE
    shard = iota((128, shards), 1).astype(jnp.float32)
    for k in range(blocks):
        cols = cols_ref[k * 128 : (k + 1) * 128, :].astype(jnp.float32)
        wanted = (shard == cols[:, 4:5]).astype(jnp.float32).astype(jnp.bfloat16)
        found = halves(dot(wanted, wide(table_ref[:, k, :])))
        partner = jnp.where(lane == base + cols[:, 5:6].astype(jnp.int32), found, 0.0)
        own = jnp.where(lane == row, mine_ref[k : k + 1, :], 0.0)
        error = jax.nn.sigmoid(jnp.sum(partner + own, axis=1, keepdims=True)) - cols[:, 6:7]
        part = error * feats[k * 128 : (k + 1) * 128].astype(jnp.float32) * width**-0.5
        grad_ref[k * 128 : (k + 1) * 128, :] = part.astype(jnp.bfloat16)
    return dot(turned_ref[...], grad_ref[...])


def step_kernel(
    step_no, carried_ref, rows_ref, table_ref, mine_ref, cols_ref, got_ref, turned_ref, next_counts_ref,
    new_rows_ref, new_mine_ref, sent_ref, grad_ref,
):
    act_rows, width = new_rows_ref.shape
    row_grad = gradient(step_no, table_ref, mine_ref, cols_ref, got_ref, turned_ref, grad_ref)
    rows = rows_ref[:act_rows, :] - step_rate * (weight_column(carried_ref, step_no, act_rows) * row_grad)
    new_rows_ref[...] = rows
    weighted = weight_column(carried_ref, step_no + 1, act_rows) * rows
    forward(wide(weighted), next_counts_ref[...], got_ref[:, step_no + 1].reshape(-1, width), new_mine_ref, sent_ref)


def last_kernel(
    step_no, me_ref, slot_ref, carried_ref, rows_ref, table_ref, mine_ref, cols_ref, got_ref, turned_ref,
    *refs,
):
    *known_refs, back_ref, grad_ref = refs
    act_rows = rows_ref.shape[0]
    row_grad = gradient(step_no, table_ref, mine_ref, cols_ref, got_ref, turned_ref, grad_ref)
    rows = rows_ref[...] - step_rate * (weight_column(carried_ref, step_no, act_rows) * row_grad)
    back_ref[:act_rows, :] = (rows - carried_ref[:act_rows, :]).astype(jnp.bfloat16)
    logits = own_logits(me_ref[0], table_ref, slot_ref[step_no])
    logits = jnp.concatenate([ref[...] for ref in known_refs] + [logits], axis=0)
    terms = [term.astype(jnp.float32) for term in split3(logits)]
    back_ref[act_rows:, :] = jnp.concatenate(terms + [jnp.zeros_like(logits)], axis=0).astype(jnp.bfloat16)


def call(kernel, args, outs, scratch=()):
    smem, vmem = (pl.BlockSpec(memory_space=space) for space in (pltpu.SMEM, pltpu.VMEM))
    return pl.pallas_call(
        kernel,
        in_specs=[smem if arg.size == 1 else vmem for arg in args],
        out_specs=[vmem] * len(outs),
        out_shape=list(outs),
        scratch_shapes=list(scratch),
        compiler_params=pltpu.CompilerParams(vmem_limit_bytes=VMEM_LIMIT),
    )(*args)


def merge_kernel(blocks_ref, here_ref, table_ref, near_ref, far_ref, other_near_ref, other_far_ref, out_ref,
    sum_ref, new_ref, sem, out_sems,
):
    places, act_rows, _ = near_ref.shape
    places = 2 * places
    active = act_rows // BLK
    groups = 2 * places
    low = here_ref[0] == 0
    copy = pltpu.make_async_copy(table_ref, new_ref, sem)
    copy.start()
    sum_ref[...] = jnp.zeros_like(sum_ref)

    def one(place, carry):
        apart = place ^ here_ref[1]
        part = ((apart >> 2) & 1) | (apart & 2)
        near = (apart & 1) == 0
        for c in range(2):
            own = low if c == 0 else jnp.logical_not(low)
            spots, values = [], []
            for slot in range(active):
                at = pl.ds(slot * BLK, BLK)
                mine = jnp.where(near, near_ref[part, at, :], far_ref[part, at, :])
                other = jnp.where(near, other_near_ref[part, at, :], other_far_ref[part, at, :])
                value = jnp.where(own, mine, other).astype(jnp.float32)
                spot = pl.ds(pl.multiple_of(blocks_ref[2 * place + c, slot] * BLK, BLK), BLK)
                spots.append(spot)
                values.append(sum_ref[spot, :] + value)
            for spot, value in zip(spots, values):
                sum_ref[spot, :] = value
        return carry

    lax.fori_loop(0, places, one, 0)
    copy.wait()
    chunks = out_sems.shape[0]
    size = out_ref.shape[0] // chunks
    outs = []
    for n in range(chunks):
        part = pl.ds(n * size, size)
        new_ref[part, :] = new_ref[part, :] + sum_ref[part, :] * (1.0 / groups)
        outs.append(pltpu.make_async_copy(new_ref.at[part], out_ref.at[part], out_sems.at[n]))
        outs[-1].start()
    for out in outs:
        out.wait()


def merge(blocks, here, table, held):
    smem, hbm = (pl.BlockSpec(memory_space=space) for space in (pltpu.SMEM, pltpu.HBM))
    whole = pl.BlockSpec(memory_space=pltpu.VMEM)
    return pl.pallas_call(
        merge_kernel,
        grid=(1,),
        in_specs=[smem, smem, hbm] + [whole] * 4,
        out_specs=hbm,
        out_shape=jax.ShapeDtypeStruct(table.shape, jnp.float32),
        scratch_shapes=[
            pltpu.VMEM(table.shape, jnp.float32),
            pltpu.VMEM(table.shape, jnp.float32),
            pltpu.SemaphoreType.DMA,
            pltpu.SemaphoreType.DMA((8,)),
        ],
        compiler_params=pltpu.CompilerParams(vmem_limit_bytes=MERGE_LIMIT),
    )(blocks, here, table, *held)


def body(turn, sizes, emb_table, active_blocks, hit_shards, lookup_slot, lookup_offset, block_weight, dense_feat, labels):
    shards = sizes["x"] * sizes["h"] * sizes["y"]
    _, steps, samples, _ = hit_shards.shape
    width = emb_table.shape[1]
    active = active_blocks.shape[2]
    act_rows = active * BLK
    slots = shards * STRIDE
    within = jnp.arange(BLK, dtype=jnp.int32)

    there = functools.partial(lax.ppermute, axis_name=HOME, perm=turn)
    feats = there(dense_feat[0])
    looked = (lookup_slot[0] * BLK + lookup_offset[0] + 1).transpose(2, 3, 0, 1).reshape(-1, steps, samples)
    meta = jnp.concatenate([hit_shards[0].transpose(2, 0, 1), looked, labels[0][None]], axis=0)
    meta = meta.reshape(-1, width).astype(jnp.bfloat16)
    my_blocks = active_blocks[lax.axis_index(("a1", "a0", "b", "c")), 0]
    local_index = (my_blocks[:, None] * BLK + within[None, :]).reshape(-1)
    weights = jnp.pad(block_weight[0, :, 0], ((0, 0), (0, width - active)))
    parts = [meta]
    for exact in (weights, emb_table[local_index]):
        high = lax.reduce_precision(exact, 8, 7)
        parts += [high.astype(jnp.bfloat16), (exact - high).astype(jnp.bfloat16)]
    rest = there(jnp.concatenate(parts, axis=0))
    feats, rest = lax.optimization_barrier((feats, rest))
    ends = [sum(part.shape[0] for part in parts[: n + 1]) for n in range(len(parts) - 1)]
    meta, *terms = [part.astype(jnp.float32) for part in jnp.split(rest, ends)]
    meta = meta.astype(jnp.bfloat16)
    weights = jnp.pad(terms[0] + terms[1], ((0, 8 - steps), (0, 0)))
    carried = jnp.concatenate([terms[2] + terms[3], weights], axis=0)

    packed, slot_of = pack(meta, feats, shards)
    got = lax.all_to_all(packed, GROUP, 0, 0, tiled=True)

    logit_rows = steps * samples // 128
    rows_like = jax.ShapeDtypeStruct((act_rows, width), jnp.float32)
    mine_like = jax.ShapeDtypeStruct((slots // 128, 128), jnp.float32)
    sent_like = jax.ShapeDtypeStruct((shards, slots // 128, 128), jnp.float32)
    back_like = jax.ShapeDtypeStruct((act_rows + 4 * logit_rows, width), jnp.bfloat16)
    scratch = [pltpu.VMEM((slots, width), jnp.bfloat16)]
    me = lax.axis_index(GROUP)[None]
    rows = carried
    weighted_like = jax.ShapeDtypeStruct((act_rows, 2 * width), jnp.bfloat16)
    (weighted,) = call(weigh_kernel, [carried], [weighted_like])
    mine, sent = call(first_kernel, [weighted, got], [mine_like, sent_like])
    table, known = None, []
    for t in range(steps):
        turned, cols, *more = prep(me, slot_of, got, table, t, act_rows)
        known += more[1:] if t + 1 < steps else more
        table = lax.all_to_all(sent, GROUP, 0, 0, tiled=True)
        if t + 1 < steps:
            rows, mine, sent = call(
                functools.partial(step_kernel, t),
                [carried, rows, table, mine, cols, got, turned, more[0]],
                [rows_like, mine_like, sent_like],
                scratch,
            )
        else:
            (back,) = call(
                functools.partial(last_kernel, t),
                [me, slot_of, carried, rows, table, mine, cols, got, turned, *known],
                [back_like],
                scratch,
            )

    back = there(back)
    delta, terms = back[:act_rows], back[act_rows:].astype(jnp.float32).reshape(4, logit_rows, 128)
    swap = [(0, 1), (1, 0)]
    for axis in ("a1", "a0"):
        delta = jnp.concatenate([delta, lax.ppermute(delta, axis, swap)], axis=0)
    held = [delta, lax.ppermute(delta, "b", swap)]
    held = [part.reshape(-1, act_rows, width) for part in held + [lax.ppermute(part, "c", swap) for part in held]]
    here = jnp.stack([lax.axis_index("c"), lax.axis_index(("a1", "a0", "b"))])
    new_table = merge(active_blocks[:, 0], here, emb_table, held)
    logits = (terms[0] + terms[1] + terms[2]).reshape(steps, samples)
    return new_table, logits[None]


def solution(mesh):
    shards = mesh.shape["shard"]
    y = min(4, shards // 4)
    sizes = {"a1": 2, "a0": 2, "b": 2, "c": 2, "x": shards // 4 // y, "h": 4, "y": y}
    finer = Mesh(mesh.devices.reshape(tuple(sizes.values())), tuple(sizes))
    index = lambda a, b, c, h: ((a * 2 + b) * 2 + c) * 4 + h
    turn = [
        (index(a, b, c, h), index(a ^ 2, h // 2, h % 2, b * 2 + c))
        for a in range(4)
        for b in range(2)
        for c in range(2)
        for h in range(4)
    ]
    group, shard = ("a1", "a0", "b", "c"), ("x", "h", "y")
    placed = (
        P(shard, None),
        P(None, shard, None),
        P(group, None, shard, None),
        P(group, None, shard, None, None),
        P(group, None, shard, None, None),
        P(group, None, shard, None),
        P(group, None, shard, None),
        P(group, None, shard),
    )
    return jax.shard_map(
        functools.partial(body, turn, sizes),
        mesh=finer,
        in_specs=placed,
        out_specs=(P(shard, None), P(group, None, shard)),
        check_vma=False,
    )
```
